256 devices in a mesh: gx: 64 (over z, x, core), gy: 4 (over y).
Axes of the slice: x: 4, y: 4, z: 8, core: 2. Of those that a mesh axis runs over, the one named last changes fastest.
Arguments:
- positions: float32 [3, 262144], P(None, 'gx'), may hold values from -6 to 6
- strengths: float32 [3, 262144], P(None, 'gx'), may hold values from -4 to 4
- core_radii: float32 [262144], P('gx'), may hold values from 0.1 to 0.4
- tile_pairs: int32 [2048, 2], replicated, may hold values from 0 to 255, as said below
- block_home: int32 [256], replicated, may hold values from 0 to 255, as said below
Outputs:
- velocity: float32 [3, 262144], P(None, 'gx')
- stretching: float32 [3, 262144], P(None, 'gx')
The draws below stay inside these ranges and needn't reach their ends.
Inputs may be any that keep to these rules, and one draw needn't show every extreme that they name: `tile_pairs`: each row names two different logical blocks, the smaller first. The 8 rows of one device name 16 distinct logical blocks, and at most 1 of them are stored on one gx index (storage block s is held by gx index s // 4); some gx index holds 1 of them for every device. `block_home`: A permutation of the blocks. The particles stay sharded because they are the wake solver's distributed state, and the listed pairs are the near-field part of a tree-code evaluation.
All inputs are finite; a program needn't handle non-finite values.
Results may differ from the reference program's by a relative error of at most 0.0003.
Values sent between devices are 32-bit elements; how exact they have to be, the bound alone decides.
A program may use at most 64 MiB of HBM per device.

```python
import math
import jax
import jax.numpy as jnp
from jax import lax

BS = 1024
BLK_DEV = 4
TILES_DEV = 8
NB = 256
PARTICLES = 262144
CAP = 1
N_GX = 64
N_GY = 4


def shared_layout(key):
    block_home = jax.random.permutation(jax.random.fold_in(key, 11), NB).astype(jnp.int32)
    at_storage = jnp.argsort(block_home).astype(jnp.int32)
    device_keys = jax.random.split(jax.random.fold_in(key, 12), N_GX * N_GY)

    def one_device(device_key):
        slot_key, shift_key = jax.random.split(device_key)
        slots = jax.random.permutation(slot_key, N_GX * CAP)[:2 * TILES_DEV].astype(jnp.int32)
        holders = slots // CAP
        within = slots % CAP
        shifts = jax.random.randint(shift_key, (N_GX,), 0, BLK_DEV).astype(jnp.int32)
        storage = holders * BLK_DEV + (within + shifts[holders]) % BLK_DEV
        logical = at_storage[storage].reshape(TILES_DEV, 2)
        return jnp.stack([jnp.min(logical, axis=1), jnp.max(logical, axis=1)], 1)
    tile_pairs = jax.vmap(one_device)(device_keys).reshape(N_GX * N_GY * TILES_DEV, 2)
    return (tile_pairs.astype(jnp.int32), block_home)


def draw_tile_pairs(key, part):
    return shared_layout(key)[0]


def draw_block_home(key, part):
    return shared_layout(key)[1]


def level_of(stream_key, dims, cuts, smallest, largest):
    level = 1.0
    for axis_at, parts in cuts:
        steps = jax.random.uniform(jax.random.fold_in(jax.random.fold_in(stream_key, 6), axis_at), (parts,), jnp.float32, smallest / len(cuts), largest / len(cuts))
        level = level * jnp.repeat(jnp.exp(steps), dims[axis_at] // parts).reshape((-1,) + (1,) * (len(dims) - 1 - axis_at))
    return level


def normal_values(own_key, shape, width, limit, cuts=(), dtype=jnp.bfloat16):
    loudness = level_of(own_key, shape, cuts, -0.22, 0.18) if cuts else 1.0
    drawn = jax.random.normal(own_key, shape, jnp.float32) * width * loudness
    return jnp.minimum(jnp.maximum(drawn, -limit), limit).astype(dtype)


def setup_inputs(seed: int = 0) -> dict:
    splits = jax.random.split(jax.random.key(seed), 6)
    return {
        "positions": normal_values(splits[0], (3, PARTICLES), 1.0, 6.0, ((1, 64),), jnp.float32),
        "strengths": normal_values(splits[1], (3, PARTICLES), 0.3, 4.0, ((1, 64),), jnp.float32),
        "core_radii": jnp.clip(jnp.exp(math.log(0.4) - 1.3862944 * jax.random.uniform(splits[2], (PARTICLES,), jnp.float32) ** level_of(splits[2], (PARTICLES,), ((0, 64),), -0.2, 0.2)), 0.1, 0.4),
        "tile_pairs": draw_tile_pairs(jax.random.fold_in(splits[5], 71), 0),
        "block_home": draw_block_home(jax.random.fold_in(splits[5], 71), 0),
    }


inv_four_pi = 0.07957747154594767

def cross_product(a, b):
    return (a[1] * b[2] - a[2] * b[1], a[2] * b[0] - a[0] * b[2], a[0] * b[1] - a[1] * b[0])

def tile_rates(first, second):
    x_first = [first[k][:, None] for k in range(3)]
    w_first = [first[3 + k][:, None] for k in range(3)]
    sigma_first = first[6][:, None]
    x_second = [second[k][None, :] for k in range(3)]
    w_second = [second[3 + k][None, :] for k in range(3)]
    sigma_second = second[6][None, :]
    r = [x_first[k] - x_second[k] for k in range(3)]
    g = r[0] * r[0] + r[1] * r[1] + r[2] * r[2] + 0.5 * (sigma_first * sigma_first + sigma_second * sigma_second)
    q = lax.rsqrt(g)
    f = -inv_four_pi * q * q * q
    h = -3.0 * f * q * q
    turn_second = cross_product(r, w_second)
    turn_first = cross_product(r, w_first)
    spin = cross_product(w_first, w_second)
    along_first = r[0] * w_first[0] + r[1] * w_first[1] + r[2] * w_first[2]
    along_second = r[0] * w_second[0] + r[1] * w_second[1] + r[2] * w_second[2]
    rates_first = [lax.optimization_barrier(jnp.sum(f * turn_second[k], axis=1)) for k in range(3)]
    rates_first = rates_first + [lax.optimization_barrier(jnp.sum(f * spin[k] + h * along_first * turn_second[k], axis=1)) for k in range(3)]
    rates_second = [-lax.optimization_barrier(jnp.sum(f * turn_first[k], axis=0)) for k in range(3)]
    rates_second = rates_second + [lax.optimization_barrier(jnp.sum(h * along_second * turn_first[k] - f * spin[k], axis=0)) for k in range(3)]
    return (jnp.stack(rates_first), jnp.stack(rates_second))

def reference(positions, strengths, core_radii, tile_pairs, block_home):
    packed = jnp.concatenate([positions, strengths, core_radii[None, :]], 0).reshape(7, NB, BS)
    stored = block_home[tile_pairs].astype(jnp.int32)

    def step(totals, pair):
        first = lax.dynamic_index_in_dim(packed, pair[0], 1, keepdims=False)
        second = lax.dynamic_index_in_dim(packed, pair[1], 1, keepdims=False)
        gained_first, gained_second = tile_rates(first, second)
        totals = totals.at[:, pair[0]].add(gained_first)
        totals = totals.at[:, pair[1]].add(gained_second)
        return (totals, None)
    totals = lax.scan(step, jnp.zeros((6, NB, BS), jnp.float32), stored)[0]
    totals = totals.reshape(6, NB * BS)
    return (totals[:3], totals[3:])
```

```python
import functools

import jax
import jax.numpy as jnp
from jax import lax
from jax.experimental import pallas as pl
from jax.experimental.pallas import tpu as pltpu
from jax.sharding import PartitionSpec as P

BS = 1024
TILES_DEV = 8
BLK_DEV = 4
N_Z, N_X, N_CORE, N_Y = 8, 4, 2, 4
TEAM = N_CORE * N_Y
SLOTS = 2 * TILES_DEV
NB = 256
ROW = BLK_DEV * N_CORE * N_X
LANES = 128
MESH = pl.DeviceIdType.MESH

inv_four_pi = 0.07957747154594767
f32, bf16 = jnp.float32, jnp.bfloat16
NT = (((1,), (1,)), ((), ()))
NN = (((1,), (0,)), ((), ()))


def split3(a):
    hi = a.astype(bf16)
    rest = a - hi.astype(f32)
    mid = rest.astype(bf16)
    lo = (rest - mid.astype(f32)).astype(bf16)
    return hi, mid, lo


def split2(v):
    hi = v.astype(bf16)
    return hi, (v - hi.astype(f32)).astype(bf16)


def cross_rows(a, b):
    a0, a1, a2 = (a[k : k + 1] for k in range(3))
    b0, b1, b2 = (b[k : k + 1] for k in range(3))
    return jnp.concatenate([a1 * b2 - a2 * b1, a2 * b0 - a0 * b2, a0 * b1 - a1 * b0], 0)


def moments(x, w):
    base = jnp.concatenate([w, cross_rows(x, w), jnp.zeros((2, w.shape[1]), f32)], 0)
    parts = [base] + [x[k : k + 1] * base for k in range(3)]
    full = split3(jnp.concatenate(parts, 0))
    return jnp.concatenate([s[:8] for s in full], 0), jnp.concatenate(full, 0)


def gains(x, w, a, s):
    a = a[0:8] + (a[8:16] + a[16:24])
    s = s[0:32] + (s[32:64] + s[64:96])
    along = x[0:1] * w[0:1] + x[1:2] * w[1:2] + x[2:3] * w[2:3]
    t = along * s[0:8] - (w[0:1] * s[8:16] + w[1:2] * s[16:24] + w[2:3] * s[24:32])
    vel = (cross_rows(x, a[0:3]) - a[3:6]) * -inv_four_pi
    turn = cross_rows(x, t[0:3]) - t[3:6]
    stretch = (3.0 * inv_four_pi) * turn - inv_four_pi * cross_rows(w, a[0:3])
    return vel, stretch


def tile_rates(first, second, piece):
    n = first.shape[1]
    total = jnp.sum(first[0:3], axis=1, keepdims=True) + jnp.sum(second[0:3], axis=1, keepdims=True)
    centre = total * (0.5 / n)
    xp, xq = first[0:3] - centre, second[0:3] - centre
    wp, wq = first[3:6], second[3:6]
    sp, sq = 0.5 * first[6:7] * first[6:7], 0.5 * second[6:7] * second[6:7]
    bp, mp = moments(xp, wp)
    bq, mq = moments(xq, wq)
    cols = jnp.transpose(jnp.concatenate([first[0:3], sp, first[4:8]], 0))
    aq = jnp.zeros((24, n), f32)
    hq = jnp.zeros((96, n), f32)
    ap, hp = [], []
    dot = functools.partial(lax.dot_general, preferred_element_type=f32)
    for s in range(0, n, piece):
        cs = cols[s : s + piece]
        r = [cs[:, k : k + 1] - second[k : k + 1] for k in range(3)]
        g = r[0] * r[0] + r[1] * r[1] + r[2] * r[2] + (cs[:, 3:4] + sq)
        q = lax.rsqrt(g)
        q2 = q * q
        f = q2 * q
        h = f * q2
        fh, fl = split2(f)
        hh, hl = split2(h)
        ap.append(dot(fh, bq, NT) + dot(fl, bq, NT))
        hp.append(dot(hh, mq, NT) + dot(hl, mq, NT))
        bps, mps = bp[:, s : s + piece], mp[:, s : s + piece]
        aq = aq + (dot(bps, fh, NN) + dot(bps, fl, NN))
        hq = hq + (dot(mps, hh, NN) + dot(mps, hl, NN))
    ap, hp = jnp.transpose(jnp.concatenate(ap, 0)), jnp.transpose(jnp.concatenate(hp, 0))
    return gains(xp, wp, ap, hp) + gains(xq, wq, aq, hq)


def pairs_kernel(in_ref, out_ref):
    def step(t, _):
        def rows(s):
            return jnp.concatenate([in_ref[e, s] for e in range(TEAM)], 1)

        v1, s1, v2, s2 = tile_rates(rows(2 * t), rows(2 * t + 1), 128)
        for s, v, st in ((2 * t, v1, s1), (2 * t + 1, v2, s2)):
            full = jnp.concatenate([v, st, jnp.zeros((2, v.shape[1]), f32)], 0)
            for e in range(TEAM):
                out_ref[e, s] = full[:, LANES * e : LANES * (e + 1)]
        return 0

    lax.fori_loop(0, TILES_DEV, step, 0)


def pairs(blocks):
    return pl.pallas_call(
        pairs_kernel,
        out_shape=jax.ShapeDtypeStruct((TEAM, SLOTS, 8, LANES), f32),
        in_specs=[pl.BlockSpec(memory_space=pltpu.VMEM)],
        out_specs=pl.BlockSpec(memory_space=pltpu.VMEM),
        compiler_params=pltpu.CompilerParams(vmem_limit_bytes=48 * 2**20),
    )(blocks)


def place():
    gx, y = lax.axis_index("gx"), lax.axis_index("gy")
    core = lax.rem(gx, 2)
    x = lax.rem(gx // 2, N_X)
    z = gx // (2 * N_X)
    return z, x, core, y


def gx_of(z, x, core):
    return (z * N_X + x) * 2 + core


def wrap(v, n):
    return lax.rem(v + n, n)


X_OFFSETS = [(0, 1), (1, 0), (3, 0), (1, 1), (3, 1), (2, 0), (2, 1)]
TEAM_OFFSETS = [(0, 1), (1, 0), (3, 0), (1, 1), (3, 1), (2, 0), (2, 1)]


def flip(core, d):
    return core if d == 0 else 1 - core


def greet(z, x, core, y):
    barrier = pltpu.get_barrier_semaphore()
    there = [(gx_of(z, wrap(x + dx, N_X), flip(core, dc)), y) for dx, dc in X_OFFSETS]
    there += [(gx_of(wrap(z + dz, N_Z), x, core), y) for dz in (1, -1)]
    there += [(gx_of(z, x, flip(core, dc)), wrap(y + dy, N_Y)) for dy, dc in TEAM_OFFSETS if dy]
    for device in there:
        pl.semaphore_signal(barrier, inc=1, device_id=device, device_id_type=MESH)
    pl.semaphore_wait(barrier, len(there))


def remote(src, dst, send, recv, device):
    return pltpu.make_async_remote_copy(
        src_ref=src, dst_ref=dst, send_sem=send, recv_sem=recv, device_id=device, device_id_type=MESH
    )


def gather_kernel(
    ids_ref, pos_ref, str_ref, rad_ref, out_ref, own, grid, pack, xs, xr, zs, zr, ts, tr
):
    z, x, core, y = place()
    gx = gx_of(z, x, core)
    me = core * N_Y + y
    for c in range(N_CORE):
        for b in range(BLK_DEV):
            at = pl.ds(pl.multiple_of(b * BS + (c * N_Y + y) * LANES, LANES), LANES)
            own[c, b] = jnp.zeros((8, LANES), f32)
            own[c, b, 0:3, :] = pos_ref[:, at]
            own[c, b, 3:6, :] = str_ref[:, at]
            own[c, b, 6:7, :] = rad_ref[:, at]
    greet(z, x, core, y)

    def mine(first):
        return grid.at[pl.ds(first * BLK_DEV, BLK_DEV)]

    copies = []
    for i, (dx, dc) in enumerate(X_OFFSETS):
        there = flip(core, dc)
        to = (gx_of(z, wrap(x + dx, N_X), there), y)
        copy = remote(own.at[there], mine(gx), xs.at[i], xr.at[i], to)
        copy.start()
        copies.append(copy)
    for b in range(BLK_DEV):
        grid[gx * BLK_DEV + b] = own[core, b]

    def piece(row, u):
        return grid.at[pl.ds((row * N_X + wrap(x + u, N_X)) * 2 * BLK_DEV, 2 * BLK_DEV)]

    def along(way, s, u):
        row = wrap(z - s, N_Z) if way == 0 else wrap(z + s, N_Z)
        to = (gx_of(wrap(z + (1 if way == 0 else -1), N_Z), x, core), y)
        return remote(piece(row, u), piece(row, u), zs.at[way, s, u], zr.at[way, s, u], to)

    def arrived(way, s, u):
        row = wrap(z - s - 1, N_Z) if way == 0 else wrap(z + s + 1, N_Z)
        return remote(
            piece(row, u), piece(row, u), zs.at[way, s, u], zr.at[way, s, u], (gx, wrap(y + 1, N_Y))
        )

    def x_arrived(i):
        dx, dc = X_OFFSETS[i]
        source = gx_of(z, wrap(x - dx, N_X), flip(core, dc))
        remote(own.at[0], mine(source), xs.at[i], xr.at[i], (gx, wrap(y + 1, N_Y))).wait_recv()

    order = {0: [0], 3: [1, 3], 1: [2, 4], 2: [5, 6]}
    last = {0: (0, 1), 1: (2, 3)}
    sends = []
    for s in range(4):
        for u, needs in order.items():
            if s == 0:
                for i in needs:
                    x_arrived(i)
            for way in (0, 1):
                if s == 3 and u not in last[way]:
                    continue
                if s:
                    arrived(way, s - 1, u).wait_recv()
                copy = along(way, s, u)
                copy.start()
                sends.append(copy)
    for way in (0, 1):
        for u in range(4):
            if u not in last[way]:
                arrived(way, 2, u).wait_recv()
        for u in last[way]:
            arrived(way, 3, u).wait_recv()

    for i, (dy, dc) in enumerate(TEAM_OFFSETS):
        there_core, there_y = flip(core, dc), wrap(y + dy, N_Y)
        member = there_core * N_Y + there_y
        for k in range(SLOTS):
            pack[i, k] = grid[ids_ref[member * SLOTS + k]]
        copy = remote(
            pack.at[i], out_ref.at[me], ts.at[i], tr.at[i], (gx_of(z, x, there_core), there_y)
        )
        copy.start()
        sends.append(copy)
    for k in range(SLOTS):
        out_ref[me, k] = grid[ids_ref[me * SLOTS + k]]
    for copy in copies + sends:
        copy.wait_send()
    for i, (dy, dc) in enumerate(TEAM_OFFSETS):
        member = flip(core, dc) * N_Y + wrap(y - dy, N_Y)
        remote(
            pack.at[i], out_ref.at[member], ts.at[i], tr.at[i], (gx, wrap(y + 1, N_Y))
        ).wait_recv()


def gather(ids, positions, strengths, radii):
    vmem = pl.BlockSpec(memory_space=pltpu.VMEM)
    dma = pltpu.SemaphoreType.DMA
    return pl.pallas_call(
        gather_kernel,
        out_shape=jax.ShapeDtypeStruct((TEAM, SLOTS, 8, LANES), f32),
        in_specs=[pl.BlockSpec(memory_space=pltpu.SMEM)] + [vmem] * 3,
        out_specs=vmem,
        scratch_shapes=[
            pltpu.VMEM((N_CORE, BLK_DEV, 8, LANES), f32),
            pltpu.VMEM((NB, 8, LANES), f32),
            pltpu.VMEM((7, SLOTS, 8, LANES), f32),
            dma((7,)),
            dma((7,)),
            dma((2, 4, 4)),
            dma((2, 4, 4)),
            dma((7,)),
            dma((7,)),
        ],
        compiler_params=pltpu.CompilerParams(
            collective_id=0, has_side_effects=True, vmem_limit_bytes=32 * 2**20
        ),
    )(ids, positions, strengths, radii)


def reduce_kernel(
    at_ref, part_ref, vel_ref, str_ref, team, dense, zin, xin, fin, ts, tr, zs, zr, xs, xr, ys, yr
):
    z, x, core, y = place()
    gx = gx_of(z, x, core)
    me = core * N_Y + y
    other = (gx, wrap(y + 1, N_Y))
    greet(z, x, core, y)
    sends = []
    for i, (dy, dc) in enumerate(TEAM_OFFSETS):
        there_core, there_y = flip(core, dc), wrap(y + dy, N_Y)
        copy = remote(
            part_ref.at[there_core * N_Y + there_y],
            team.at[pl.ds(me * (SLOTS + 1), SLOTS)],
            ts.at[i],
            tr.at[i],
            (gx_of(z, x, there_core), there_y),
        )
        copy.start()
        sends.append(copy)
    for m in range(TEAM):
        team[m * (SLOTS + 1) + SLOTS] = jnp.zeros((8, LANES), f32)
    for k in range(SLOTS):
        team[me * (SLOTS + 1) + k] = part_ref[me, k]
    for i, (dy, dc) in enumerate(TEAM_OFFSETS):
        member = flip(core, dc) * N_Y + wrap(y - dy, N_Y)
        remote(
            part_ref.at[0], team.at[pl.ds(member * (SLOTS + 1), SLOTS)], ts.at[i], tr.at[i], other
        ).wait_recv()

    def fill(row, u):
        first = (row * N_X + wrap(x + u, N_X)) * 2 * BLK_DEV

        def one(j, _):
            b = first + j
            terms = [team[at_ref[m * NB + b]] for m in range(TEAM)]
            while len(terms) > 1:
                terms = [terms[k] + terms[k + 1] for k in range(0, len(terms), 2)]
            dense[b] = terms[0]
            return 0

        lax.fori_loop(0, 2 * BLK_DEV, one, 0, unroll=True)

    def piece(row, u):
        return dense.at[pl.ds((row * N_X + wrap(x + u, N_X)) * 2 * BLK_DEV, 2 * BLK_DEV)]

    def add(row, u, way, s):
        first = (row * N_X + wrap(x + u, N_X)) * 2 * BLK_DEV
        for j in range(2 * BLK_DEV):
            dense[first + j] = dense[first + j] + zin[way, s, u, j]

    def along(way, s, u):
        row = wrap(z + 4 - s, N_Z) if way == 0 else wrap(z - 4 + s, N_Z)
        to = (gx_of(wrap(z + (1 if way == 0 else -1), N_Z), x, core), y)
        return remote(piece(row, u), zin.at[way, s, u], zs.at[way, s, u], zr.at[way, s, u], to)

    def arrived(way, s, u):
        return remote(
            piece(z, u), zin.at[way, s, u], zs.at[way, s, u], zr.at[way, s, u], other
        ).wait_recv()

    first = {0: (0, 1), 1: (2, 3)}
    for s in range(4):
        if s == 0:
            for u in range(4):
                fill(wrap(z + 4, N_Z), u)
                way = 0 if u in first[0] else 1
                copy = along(way, 0, u)
                copy.start()
                sends.append(copy)
            continue
        for u in (2, 3, 0, 1):
            for way in (0, 1):
                row = wrap(z + 4 - s, N_Z) if way == 0 else wrap(z - 4 + s, N_Z)
                fill(row, u)
                if s > 1 or u in first[way]:
                    arrived(way, s - 1, u)
                    add(row, u, way, s - 1)
                copy = along(way, s, u)
                copy.start()
                sends.append(copy)
    for u in range(4):
        fill(z, u)
        for way in (0, 1):
            arrived(way, 3, u)
            add(z, u, way, 3)

    def home(first):
        return dense.at[pl.ds(first * BLK_DEV, BLK_DEV)]

    for i, (dx, dc) in enumerate(X_OFFSETS):
        there = gx_of(z, wrap(x + dx, N_X), flip(core, dc))
        copy = remote(home(there), xin.at[i], xs.at[i], xr.at[i], (there, y))
        copy.start()
        sends.append(copy)
    for i in range(7):
        remote(home(gx), xin.at[i], xs.at[i], xr.at[i], other).wait_recv()
    by_core = {d: [i for i, (_, dc) in enumerate(X_OFFSETS) if dc == d] for d in (0, 1)}
    for b in range(BLK_DEV):
        a = [xin[i, b] for i in by_core[0]]
        fin[0, core, b] = (dense[gx * BLK_DEV + b] + a[0]) + (a[1] + a[2])
        a = [xin[i, b] for i in by_core[1]]
        fin[0, 1 - core, b] = (a[0] + a[1]) + (a[2] + a[3])
    for i, dy in enumerate((1, 3, 2)):
        copy = remote(fin.at[0], fin.at[i + 1], ys.at[i], yr.at[i], (gx, wrap(y + dy, N_Y)))
        copy.start()
        sends.append(copy)

    def write(slot, there_y):
        for c in range(N_CORE):
            for b in range(BLK_DEV):
                at = pl.ds(pl.multiple_of(b * BS + (c * N_Y + there_y) * LANES, LANES), LANES)
                full = fin[slot, c, b]
                vel_ref[:, at] = full[0:3]
                str_ref[:, at] = full[3:6]

    write(0, y)
    for i, dy in enumerate((1, 3, 2)):
        remote(fin.at[0], fin.at[i + 1], ys.at[i], yr.at[i], other).wait_recv()
        write(i + 1, wrap(y - dy, N_Y))
    for copy in sends:
        copy.wait_send()


def reduce(at, partials):
    vmem = pl.BlockSpec(memory_space=pltpu.VMEM)
    dma = pltpu.SemaphoreType.DMA
    out = jax.ShapeDtypeStruct((3, BLK_DEV * BS), f32)
    return pl.pallas_call(
        reduce_kernel,
        out_shape=(out, out),
        in_specs=[pl.BlockSpec(memory_space=pltpu.SMEM), vmem],
        out_specs=(vmem, vmem),
        scratch_shapes=[
            pltpu.VMEM((TEAM * (SLOTS + 1), 8, LANES), f32),
            pltpu.VMEM((NB, 8, LANES), f32),
            pltpu.VMEM((2, 4, 4, 2 * BLK_DEV, 8, LANES), f32),
            pltpu.VMEM((7, BLK_DEV, 8, LANES), f32),
            pltpu.VMEM((4, N_CORE, BLK_DEV, 8, LANES), f32),
            dma((7,)),
            dma((7,)),
            dma((2, 4, 4)),
            dma((2, 4, 4)),
            dma((7,)),
            dma((7,)),
            dma((3,)),
            dma((3,)),
        ],
        compiler_params=pltpu.CompilerParams(
            collective_id=1, has_side_effects=True, vmem_limit_bytes=32 * 2**20
        ),
    )(at, partials)


def body(positions, strengths, core_radii, tile_pairs, block_home):
    chip = lax.axis_index("gx") // 2
    teams = tile_pairs.reshape(N_Z * N_X, TEAM * SLOTS)
    logical = lax.dynamic_index_in_dim(teams, chip, 0, keepdims=False)
    blocks = jnp.arange(NB, dtype=jnp.int32)
    match = logical[:, None] == blocks
    stored = jnp.sum(jnp.where(match, block_home, 0), axis=1)
    slot = jnp.arange(SLOTS, dtype=jnp.int32)[None, :, None]
    named = stored.reshape(TEAM, SLOTS, 1) == blocks
    at = jnp.min(jnp.where(named, slot, SLOTS), axis=1)
    at = at + (SLOTS + 1) * jnp.arange(TEAM, dtype=jnp.int32)[:, None]
    own_blocks = gather(stored, positions, strengths, core_radii[None, :])
    return reduce(at.reshape(-1), pairs(own_blocks))


def solution(mesh):
    return jax.shard_map(
        body,
        mesh=mesh,
        in_specs=(P(None, "gx"), P(None, "gx"), P("gx"), P(), P()),
        out_specs=(P(None, "gx"), P(None, "gx")),
        check_vma=False,
    )
```

```python
import functools

import jax
import jax.numpy as jnp
from jax import lax
from jax.experimental import pallas as pl
from jax.experimental.pallas import tpu as pltpu
from jax.sharding import PartitionSpec as P

BS = 1024
TILES_DEV = 8
BLK_DEV = 4
N_Z, N_X, N_CORE, N_Y = 8, 4, 2, 4
TEAM = N_CORE * N_Y
SLOTS = 2 * TILES_DEV
NB = 256
ROW = BLK_DEV * N_CORE * N_X
LANES = 128
MESH = pl.DeviceIdType.MESH

inv_four_pi = 0.07957747154594767
f32, bf16 = jnp.float32, jnp.bfloat16
NT = (((1,), (1,)), ((), ()))
NN = (((1,), (0,)), ((), ()))


def split3(a):
    hi = a.astype(bf16)
    rest = a - hi.astype(f32)
    mid = rest.astype(bf16)
    lo = (rest - mid.astype(f32)).astype(bf16)
    return hi, mid, lo


def split2(v):
    hi = v.astype(bf16)
    return hi, (v - hi.astype(f32)).astype(bf16)


def cross_rows(a, b):
    a0, a1, a2 = (a[k : k + 1] for k in range(3))
    b0, b1, b2 = (b[k : k + 1] for k in range(3))
    return jnp.concatenate([a1 * b2 - a2 * b1, a2 * b0 - a0 * b2, a0 * b1 - a1 * b0], 0)


def moments(x, w):
    base = jnp.concatenate([w, cross_rows(x, w), jnp.zeros((2, w.shape[1]), f32)], 0)
    parts = [base] + [x[k : k + 1] * base for k in range(3)]
    full = split3(jnp.concatenate(parts, 0))
    return jnp.concatenate([s[:8] for s in full], 0), jnp.concatenate(full, 0)


def gains(x, w, a, s):
    a = a[0:8] + (a[8:16] + a[16:24])
    s = s[0:32] + (s[32:64] + s[64:96])
    along = x[0:1] * w[0:1] + x[1:2] * w[1:2] + x[2:3] * w[2:3]
    t = along * s[0:8] - (w[0:1] * s[8:16] + w[1:2] * s[16:24] + w[2:3] * s[24:32])
    vel = (cross_rows(x, a[0:3]) - a[3:6]) * -inv_four_pi
    turn = cross_rows(x, t[0:3]) - t[3:6]
    stretch = (3.0 * inv_four_pi) * turn - inv_four_pi * cross_rows(w, a[0:3])
    return vel, stretch


def tile_rates(first, second, piece):
    n = first.shape[1]
    total = jnp.sum(first[0:3], axis=1, keepdims=True) + jnp.sum(second[0:3], axis=1, keepdims=True)
    centre = total * (0.5 / n)
    xp, xq = first[0:3] - centre, second[0:3] - centre
    wp, wq = first[3:6], second[3:6]
    sp, sq = 0.5 * first[6:7] * first[6:7], 0.5 * second[6:7] * second[6:7]
    bp, mp = moments(xp, wp)
    bq, mq = moments(xq, wq)
    cols = jnp.transpose(jnp.concatenate([first[0:3], sp, first[4:8]], 0))
    aq = jnp.zeros((24, n), f32)
    hq = jnp.zeros((96, n), f32)
    ap, hp = [], []
    dot = functools.partial(lax.dot_general, preferred_element_type=f32)
    for s in range(0, n, piece):
        cs = cols[s : s + piece]
        r = [cs[:, k : k + 1] - second[k : k + 1] for k in range(3)]
        g = r[0] * r[0] + r[1] * r[1] + r[2] * r[2] + (cs[:, 3:4] + sq)
        q = lax.rsqrt(g)
        q2 = q * q
        f = q2 * q
        h = f * q2
        fh, fl = split2(f)
        hh, hl = split2(h)
        ap.append(dot(fh, bq, NT) + dot(fl, bq, NT))
        hp.append(dot(hh, mq, NT) + dot(hl, mq, NT))
        bps, mps = bp[:, s : s + piece], mp[:, s : s + piece]
        aq = aq + (dot(bps, fh, NN) + dot(bps, fl, NN))
        hq = hq + (dot(mps, hh, NN) + dot(mps, hl, NN))
    ap, hp = jnp.transpose(jnp.concatenate(ap, 0)), jnp.transpose(jnp.concatenate(hp, 0))
    return gains(xp, wp, ap, hp) + gains(xq, wq, aq, hq)


def place():
    gx, y = lax.axis_index("gx"), lax.axis_index("gy")
    core = lax.rem(gx, 2)
    x = lax.rem(gx // 2, N_X)
    z = gx // (2 * N_X)
    return z, x, core, y


def gx_of(z, x, core):
    return (z * N_X + x) * 2 + core


def wrap(v, n):
    return lax.rem(v + n, n)


X_OFFSETS = [(0, 1), (1, 0), (3, 0), (1, 1), (3, 1), (2, 0), (2, 1)]
TEAM_OFFSETS = [(0, 1), (1, 0), (3, 0), (1, 1), (3, 1), (2, 0), (2, 1)]


def flip(core, d):
    return core if d == 0 else 1 - core


def greet(z, x, core, y):
    barrier = pltpu.get_barrier_semaphore()
    there = [(gx_of(z, wrap(x + dx, N_X), flip(core, dc)), y) for dx, dc in X_OFFSETS]
    there += [(gx_of(wrap(z + dz, N_Z), x, core), y) for dz in (1, -1)]
    there += [(gx_of(z, x, flip(core, dc)), wrap(y + dy, N_Y)) for dy, dc in TEAM_OFFSETS if dy]
    for device in there:
        pl.semaphore_signal(barrier, inc=1, device_id=device, device_id_type=MESH)
    pl.semaphore_wait(barrier, len(there))


def remote(src, dst, send, recv, device):
    return pltpu.make_async_remote_copy(
        src_ref=src, dst_ref=dst, send_sem=send, recv_sem=recv, device_id=device, device_id_type=MESH
    )


def kernel(
    ids_ref, at_ref, pos_ref, str_ref, rad_ref, vel_out, str_out,
    own, grid, pack, named, part, team, dense, zin, xin, fin,
    gxs, gxr, gzs, gzr, ts, tr, ps, pr, zs, zr, xs, xr, ys, yr,
):
    z, x, core, y = place()
    gx = gx_of(z, x, core)
    other = (gx, wrap(y + 1, N_Y))
    me = core * N_Y + y
    for c in range(N_CORE):
        for b in range(BLK_DEV):
            at = pl.ds(pl.multiple_of(b * BS + (c * N_Y + y) * LANES, LANES), LANES)
            own[c, b] = jnp.zeros((8, LANES), f32)
            own[c, b, 0:3, :] = pos_ref[:, at]
            own[c, b, 3:6, :] = str_ref[:, at]
            own[c, b, 6:7, :] = rad_ref[:, at]
    greet(z, x, core, y)

    def mine(first):
        return grid.at[pl.ds(first * BLK_DEV, BLK_DEV)]

    copies = []
    for i, (dx, dc) in enumerate(X_OFFSETS):
        there = flip(core, dc)
        to = (gx_of(z, wrap(x + dx, N_X), there), y)
        copy = remote(own.at[there], mine(gx), gxs.at[i], gxr.at[i], to)
        copy.start()
        copies.append(copy)
    for b in range(BLK_DEV):
        grid[gx * BLK_DEV + b] = own[core, b]

    def part_of(row, u):
        return grid.at[pl.ds((row * N_X + wrap(x + u, N_X)) * 2 * BLK_DEV, 2 * BLK_DEV)]

    def onward(way, s, u):
        row = wrap(z - s, N_Z) if way == 0 else wrap(z + s, N_Z)
        to = (gx_of(wrap(z + (1 if way == 0 else -1), N_Z), x, core), y)
        return remote(part_of(row, u), part_of(row, u), gzs.at[way, s, u], gzr.at[way, s, u], to)

    def came(way, s, u):
        row = wrap(z - s - 1, N_Z) if way == 0 else wrap(z + s + 1, N_Z)
        return remote(
            part_of(row, u), part_of(row, u), gzs.at[way, s, u], gzr.at[way, s, u], (gx, wrap(y + 1, N_Y))
        )

    def x_came(i):
        dx, dc = X_OFFSETS[i]
        source = gx_of(z, wrap(x - dx, N_X), flip(core, dc))
        remote(own.at[0], mine(source), gxs.at[i], gxr.at[i], (gx, wrap(y + 1, N_Y))).wait_recv()

    order = {0: [0], 3: [1, 3], 1: [2, 4], 2: [5, 6]}
    last = {0: (0, 1), 1: (2, 3)}
    sends = []
    for s in range(4):
        for u, needs in order.items():
            if s == 0:
                for i in needs:
                    x_came(i)
            for way in (0, 1):
                if s == 3 and u not in last[way]:
                    continue
                if s:
                    came(way, s - 1, u).wait_recv()
                copy = onward(way, s, u)
                copy.start()
                sends.append(copy)
    for way in (0, 1):
        for u in range(4):
            if u not in last[way]:
                came(way, 2, u).wait_recv()
        for u in last[way]:
            came(way, 3, u).wait_recv()

    def two(t):
        return pl.ds(pl.multiple_of(2 * t, 2), 2)

    def mate(i):
        dy, dc = TEAM_OFFSETS[i]
        there_core, there_y = flip(core, dc), wrap(y + dy, N_Y)
        return there_core * N_Y + there_y, (gx_of(z, x, there_core), there_y)

    def mate_from(i):
        dy, dc = TEAM_OFFSETS[i]
        return flip(core, dc) * N_Y + wrap(y - dy, N_Y)

    def ask(i, t):
        return remote(
            pack.at[i, two(t)], named.at[me, two(t)], ts.at[i, t], tr.at[i, t], mate(i)[1]
        )

    def give(i, t):
        member, to = mate(i)
        return remote(
            part.at[member, two(t)],
            team.at[pl.ds(me * (SLOTS + 1) + 2 * t, 2)],
            ps.at[i, t],
            pr.at[i, t],
            to,
        )

    def send_tile(t, _):
        for i in range(7):
            member = mate(i)[0]
            for k in (2 * t, 2 * t + 1):
                pack[i, k] = grid[ids_ref[member * SLOTS + k]]
            ask(i, t).start()
        for k in (2 * t, 2 * t + 1):
            named[me, k] = grid[ids_ref[me * SLOTS + k]]
        return 0

    lax.fori_loop(0, TILES_DEV, send_tile, 0)
    for m in range(TEAM):
        team[m * (SLOTS + 1) + SLOTS] = jnp.zeros((8, LANES), f32)

    def one_tile(t, _):
        for i in range(7):
            member = mate_from(i)
            remote(
                pack.at[i, two(t)], named.at[member, two(t)], ts.at[i, t], tr.at[i, t], other
            ).wait_recv()

        def rows(s):
            return jnp.concatenate([named[e, s] for e in range(TEAM)], 1)

        v1, s1, v2, s2 = tile_rates(rows(2 * t), rows(2 * t + 1), 128)
        for s, v, st in ((2 * t, v1, s1), (2 * t + 1, v2, s2)):
            full = jnp.concatenate([v, st, jnp.zeros((2, v.shape[1]), f32)], 0)
            for e in range(TEAM):
                part[e, s] = full[:, LANES * e : LANES * (e + 1)]
        for i in range(7):
            give(i, t).start()
        for k in (2 * t, 2 * t + 1):
            team[me * (SLOTS + 1) + k] = part[me, k]
        return 0

    lax.fori_loop(0, TILES_DEV, one_tile, 0)

    def settle(t, _):
        for i in range(7):
            ask(i, t).wait_send()
            give(i, t).wait_send()
            member = mate_from(i)
            remote(
                part.at[0, two(t)],
                team.at[pl.ds(member * (SLOTS + 1) + 2 * t, 2)],
                ps.at[i, t],
                pr.at[i, t],
                other,
            ).wait_recv()
        return 0

    lax.fori_loop(0, TILES_DEV, settle, 0)

    def fill(row, u):
        first = (row * N_X + wrap(x + u, N_X)) * 2 * BLK_DEV

        def one(j, _):
            b = first + j
            terms = [team[at_ref[m * NB + b]] for m in range(TEAM)]
            while len(terms) > 1:
                terms = [terms[k] + terms[k + 1] for k in range(0, len(terms), 2)]
            dense[b] = terms[0]
            return 0

        lax.fori_loop(0, 2 * BLK_DEV, one, 0, unroll=True)

    def piece(row, u):
        return dense.at[pl.ds((row * N_X + wrap(x + u, N_X)) * 2 * BLK_DEV, 2 * BLK_DEV)]

    def add(row, u, way, s):
        first = (row * N_X + wrap(x + u, N_X)) * 2 * BLK_DEV
        for j in range(2 * BLK_DEV):
            dense[first + j] = dense[first + j] + zin[way, s, u, j]

    def along(way, s, u):
        row = wrap(z + 4 - s, N_Z) if way == 0 else wrap(z - 4 + s, N_Z)
        to = (gx_of(wrap(z + (1 if way == 0 else -1), N_Z), x, core), y)
        return remote(piece(row, u), zin.at[way, s, u], zs.at[way, s, u], zr.at[way, s, u], to)

    def arrived(way, s, u):
        return remote(
            piece(z, u), zin.at[way, s, u], zs.at[way, s, u], zr.at[way, s, u], other
        ).wait_recv()

    early = {0: (0, 1), 1: (2, 3)}
    for s in range(4):
        if s == 0:
            for u in range(4):
                fill(wrap(z + 4, N_Z), u)
                way = 0 if u in early[0] else 1
                copy = along(way, 0, u)
                copy.start()
                sends.append(copy)
            continue
        for u in (2, 3, 0, 1):
            for way in (0, 1):
                row = wrap(z + 4 - s, N_Z) if way == 0 else wrap(z - 4 + s, N_Z)
                fill(row, u)
                if s > 1 or u in early[way]:
                    arrived(way, s - 1, u)
                    add(row, u, way, s - 1)
                copy = along(way, s, u)
                copy.start()
                sends.append(copy)
    for u in range(4):
        fill(z, u)
        for way in (0, 1):
            arrived(way, 3, u)
            add(z, u, way, 3)

    def home(first):
        return dense.at[pl.ds(first * BLK_DEV, BLK_DEV)]

    for i, (dx, dc) in enumerate(X_OFFSETS):
        there = gx_of(z, wrap(x + dx, N_X), flip(core, dc))
        copy = remote(home(there), xin.at[i], xs.at[i], xr.at[i], (there, y))
        copy.start()
        sends.append(copy)
    for i in range(7):
        remote(home(gx), xin.at[i], xs.at[i], xr.at[i], other).wait_recv()
    by_core = {d: [i for i, (_, dc) in enumerate(X_OFFSETS) if dc == d] for d in (0, 1)}
    for b in range(BLK_DEV):
        a = [xin[i, b] for i in by_core[0]]
        fin[0, core, b] = (dense[gx * BLK_DEV + b] + a[0]) + (a[1] + a[2])
        a = [xin[i, b] for i in by_core[1]]
        fin[0, 1 - core, b] = (a[0] + a[1]) + (a[2] + a[3])
    for i, dy in enumerate((1, 3, 2)):
        copy = remote(fin.at[0], fin.at[i + 1], ys.at[i], yr.at[i], (gx, wrap(y + dy, N_Y)))
        copy.start()
        sends.append(copy)

    def write(slot, there_y):
        for c in range(N_CORE):
            for b in range(BLK_DEV):
                at = pl.ds(pl.multiple_of(b * BS + (c * N_Y + there_y) * LANES, LANES), LANES)
                full = fin[slot, c, b]
                vel_out[:, at] = full[0:3]
                str_out[:, at] = full[3:6]

    write(0, y)
    for i, dy in enumerate((1, 3, 2)):
        remote(fin.at[0], fin.at[i + 1], ys.at[i], yr.at[i], other).wait_recv()
        write(i + 1, wrap(y - dy, N_Y))
    for copy in copies + sends:
        copy.wait_send()


def run(ids, at, positions, strengths, radii):
    vmem, smem = pl.BlockSpec(memory_space=pltpu.VMEM), pl.BlockSpec(memory_space=pltpu.SMEM)
    dma = pltpu.SemaphoreType.DMA
    out = jax.ShapeDtypeStruct((3, BLK_DEV * BS), f32)
    buffers = [
        (N_CORE, BLK_DEV),
        (NB,),
        (7, SLOTS),
        (TEAM, SLOTS),
        (TEAM, SLOTS),
        (TEAM * (SLOTS + 1),),
        (NB,),
        (2, 4, 4, 2 * BLK_DEV),
        (7, BLK_DEV),
        (4, N_CORE, BLK_DEV),
    ]
    counts = [(7,), (2, 4, 4), (7, TILES_DEV), (7, TILES_DEV), (2, 4, 4), (7,), (3,)]
    return pl.pallas_call(
        kernel,
        out_shape=(out, out),
        in_specs=[smem, smem, vmem, vmem, vmem],
        out_specs=(vmem, vmem),
        scratch_shapes=[pltpu.VMEM(b + (8, LANES), f32) for b in buffers]
        + [dma(c) for c in counts for _ in range(2)],
        compiler_params=pltpu.CompilerParams(
            collective_id=0, has_side_effects=True, vmem_limit_bytes=48 * 2**20
        ),
    )(ids, at, positions, strengths, radii)


def body(positions, strengths, core_radii, tile_pairs, block_home):
    chip = lax.axis_index("gx") // 2
    teams = tile_pairs.reshape(N_Z * N_X, TEAM * SLOTS)
    logical = lax.dynamic_index_in_dim(teams, chip, 0, keepdims=False)
    blocks = jnp.arange(NB, dtype=jnp.int32)
    match = logical[:, None] == blocks
    stored = jnp.sum(jnp.where(match, block_home, 0), axis=1)
    slot = jnp.arange(SLOTS, dtype=jnp.int32)[None, :, None]
    named = stored.reshape(TEAM, SLOTS, 1) == blocks
    at = jnp.min(jnp.where(named, slot, SLOTS), axis=1)
    at = at + (SLOTS + 1) * jnp.arange(TEAM, dtype=jnp.int32)[:, None]
    return run(stored, at.reshape(-1), positions, strengths, core_radii[None, :])


def solution(mesh):
    return jax.shard_map(
        body,
        mesh=mesh,
        in_specs=(P(None, "gx"), P(None, "gx"), P("gx"), P(), P()),
        out_specs=(P(None, "gx"), P(None, "gx")),
        check_vma=False,
    )
```

```python
import functools

import jax
import jax.numpy as jnp
from jax import lax
from jax.experimental import pallas as pl
from jax.experimental.pallas import tpu as pltpu
from jax.sharding import PartitionSpec as P

BS = 1024
TILES_DEV = 8
BLK_DEV = 4
N_Z, N_X, N_CORE, N_Y = 8, 4, 2, 4
EIGHTHS = N_CORE * N_Y
TEAM = N_X * EIGHTHS
SENDERS = 3 * EIGHTHS
SLOTS = 2 * TILES_DEV
NB = 256
ROW = BLK_DEV * N_CORE * N_X
EARLY = TILES_DEV - 1
LANES = 128
MESH = pl.DeviceIdType.MESH

inv_four_pi = 0.07957747154594767
f32, bf16 = jnp.float32, jnp.bfloat16
NT = (((1,), (1,)), ((), ()))
NN = (((1,), (0,)), ((), ()))


def split3(a):
    hi = a.astype(bf16)
    rest = a - hi.astype(f32)
    mid = rest.astype(bf16)
    lo = (rest - mid.astype(f32)).astype(bf16)
    return hi, mid, lo


def split2(v):
    hi = v.astype(bf16)
    return hi, (v - hi.astype(f32)).astype(bf16)


def cross_rows(a, b):
    a0, a1, a2 = (a[k : k + 1] for k in range(3))
    b0, b1, b2 = (b[k : k + 1] for k in range(3))
    return jnp.concatenate([a1 * b2 - a2 * b1, a2 * b0 - a0 * b2, a0 * b1 - a1 * b0], 0)


def moments(x, w):
    base = jnp.concatenate([w, cross_rows(x, w), jnp.zeros((2, w.shape[1]), f32)], 0)
    parts = [base] + [x[k : k + 1] * base for k in range(3)]
    full = split3(jnp.concatenate(parts, 0))
    return jnp.concatenate([s[:8] for s in full], 0), jnp.concatenate(full, 0)


def gains(x, w, a, s):
    a = a[0:8] + (a[8:16] + a[16:24])
    s = s[0:32] + (s[32:64] + s[64:96])
    along = x[0:1] * w[0:1] + x[1:2] * w[1:2] + x[2:3] * w[2:3]
    t = along * s[0:8] - (w[0:1] * s[8:16] + w[1:2] * s[16:24] + w[2:3] * s[24:32])
    vel = (cross_rows(x, a[0:3]) - a[3:6]) * -inv_four_pi
    turn = cross_rows(x, t[0:3]) - t[3:6]
    stretch = (3.0 * inv_four_pi) * turn - inv_four_pi * cross_rows(w, a[0:3])
    return vel, stretch


def tile_rates(first, second, piece):
    n = first.shape[1]
    total = jnp.sum(first[0:3], axis=1, keepdims=True) + jnp.sum(second[0:3], axis=1, keepdims=True)
    centre = total * (0.5 / n)
    xp, xq = first[0:3] - centre, second[0:3] - centre
    wp, wq = first[3:6], second[3:6]
    sp, sq = 0.5 * first[6:7] * first[6:7], 0.5 * second[6:7] * second[6:7]
    bp, mp = moments(xp, wp)
    bq, mq = moments(xq, wq)
    cols = jnp.transpose(jnp.concatenate([first[0:3], sp, first[4:8]], 0))
    aq = jnp.zeros((24, n), f32)
    hq = jnp.zeros((96, n), f32)
    ap, hp = [], []
    dot = functools.partial(lax.dot_general, preferred_element_type=f32)
    for s in range(0, n, piece):
        cs = cols[s : s + piece]
        r = [cs[:, k : k + 1] - second[k : k + 1] for k in range(3)]
        g = r[0] * r[0] + r[1] * r[1] + r[2] * r[2] + (cs[:, 3:4] + sq)
        q = lax.rsqrt(g)
        q2 = q * q
        f = q2 * q
        h = f * q2
        fh, fl = split2(f)
        hh, hl = split2(h)
        ap.append(dot(fh, bq, NT) + dot(fl, bq, NT))
        hp.append(dot(hh, mq, NT) + dot(hl, mq, NT))
        bps, mps = bp[:, s : s + piece], mp[:, s : s + piece]
        aq = aq + (dot(bps, fh, NN) + dot(bps, fl, NN))
        hq = hq + (dot(mps, hh, NN) + dot(mps, hl, NN))
    ap, hp = jnp.transpose(jnp.concatenate(ap, 0)), jnp.transpose(jnp.concatenate(hp, 0))
    return gains(xp, wp, ap, hp) + gains(xq, wq, aq, hq)


def place():
    gx, y = lax.axis_index("gx"), lax.axis_index("gy")
    core = lax.rem(gx, 2)
    x = lax.rem(gx // 2, N_X)
    z = gx // (2 * N_X)
    return z, x, core, y


def gx_of(z, x, core):
    return (z * N_X + x) * 2 + core


def wrap(v, n):
    return lax.rem(v + n, n)


X_OFFSETS = [(2, 0), (2, 1), (1, 0), (3, 0), (1, 1), (3, 1), (0, 1)]
Z_OFFSETS = [4, 3, 5, 2, 6, 1, 7]


def flip(core, d):
    return lax.rem(core + d, 2)


def remote(src, dst, send, recv, device):
    return pltpu.make_async_remote_copy(
        src_ref=src, dst_ref=dst, send_sem=send, recv_sem=recv, device_id=device, device_id_type=MESH
    )


def kernel(
    ids_ref, keys_ref, pos_ref, str_ref, rad_ref, vel_out, str_out,
    own, grid, pack, named, part, team, pick, dense, zin, fin,
    xs, xr, gs, gr, ts, tr, ps, pr, zs, zr, fs, fr,
):
    z, x, core, y = place()
    gx = gx_of(z, x, core)
    me = x * EIGHTHS + core * N_Y + y
    other = (gx, wrap(y + 1, N_Y))
    active = x < 3

    def mate(i):
        tx, tc, ty = wrap(x + i // 8, N_X), flip(core, (i // 4) % 2), wrap(y + i % 4, N_Y)
        return tx, tx * EIGHTHS + tc * N_Y + ty, tx * 2 + tc, (gx_of(z, tx, tc), ty)

    def mate_from(i):
        tx, tc, ty = wrap(x - i // 8, N_X), flip(core, (i // 4) % 2), wrap(y - i % 4, N_Y)
        return tx, tx * EIGHTHS + tc * N_Y + ty

    def along_z(dz):
        return (gx_of(wrap(z + dz, N_Z), x, core), y)

    barrier = pltpu.get_barrier_semaphore()
    for dz in Z_OFFSETS:
        pl.semaphore_signal(barrier, inc=1, device_id=along_z(dz), device_id_type=MESH)
    for i in range(1, TEAM):
        pl.semaphore_signal(barrier, inc=1, device_id=mate(i)[3], device_id_type=MESH)
    rows_of = [(pos_ref, 0), (pos_ref, 1), (pos_ref, 2), (str_ref, 0), (str_ref, 1), (str_ref, 2)]
    for c in range(N_CORE):
        for b in range(BLK_DEV):
            at = pl.ds(pl.multiple_of(b * BS + (c * N_Y + y) * LANES, LANES), LANES)
            for k, (ref, row) in enumerate(rows_of + [(rad_ref, 0)]):
                own[k // 2, c, b, k % 2 : k % 2 + 1, :] = ref[row : row + 1, at]
            own[3, c, b, 1:2, :] = jnp.zeros((1, LANES), f32)
    pl.semaphore_wait(barrier, TEAM - 1 + len(Z_OFFSETS))

    def home_of(g):
        return grid.at[pl.ds(g * BLK_DEV, BLK_DEV)]

    def row_of(r):
        return grid.at[pl.ds(r * ROW, ROW)]

    sends = []
    for i, (dx, dc) in enumerate(X_OFFSETS):
        tx, tc = wrap(x + dx, N_X), flip(core, dc)
        copy = remote(own.at[tx, tc], home_of(gx), xs.at[i], xr.at[i], (gx_of(z, tx, tc), y))
        copy.start()
        sends.append(copy)
    for b in range(BLK_DEV):
        grid[gx * BLK_DEV + b] = own[x, core, b]
    for i, (dx, dc) in enumerate(X_OFFSETS):
        source = gx_of(z, wrap(x - dx, N_X), flip(core, dc))
        remote(own.at[0, 0], home_of(source), xs.at[i], xr.at[i], other).wait_recv()
    for i, dz in enumerate(Z_OFFSETS):
        copy = remote(row_of(z), row_of(z), gs.at[i], gr.at[i], along_z(dz))
        copy.start()
        sends.append(copy)
    for i, dz in enumerate(Z_OFFSETS):
        row = row_of(wrap(z - dz, N_Z))
        remote(row, row, gs.at[i], gr.at[i], other).wait_recv()

    parts = ((0, 1), (1, EARLY))

    def ask(i, g):
        at = pl.ds(*parts[g])
        return remote(pack.at[i, at], named.at[me, at], ts.at[g, i], tr.at[g, i], mate(i)[3])

    def asked(i, g):
        at = pl.ds(*parts[g])
        member = mate_from(i)[1]
        return remote(pack.at[i, at], named.at[member, at], ts.at[g, i], tr.at[g, i], other)

    for g, (t0, count) in enumerate(parts):

        def send(i, _, g=g, t0=t0, count=count):
            member = mate(i)[1]
            for t in range(t0, t0 + count):
                for k in range(2):
                    block = ids_ref[member * SLOTS + 2 * t + k]
                    pack[i, t, 2 * k : 2 * k + 2, :] = grid[block]
            ask(i, g).start()
            return 0

        lax.fori_loop(1, TEAM, send, 0)
    for t in range(TILES_DEV):
        for k in range(2):
            named[me, t, 2 * k : 2 * k + 2, :] = grid[ids_ref[me * SLOTS + 2 * t + k]]

    lots = ((0, EARLY), (EARLY, 1))

    def give(i, g):
        at = pl.ds(*lots[g])
        _, member, _, to = mate(i)
        return remote(part.at[member, at], team.at[me, at], ps.at[g, i], pr.at[g, i], to)

    def given(i, g):
        at = pl.ds(*lots[g])
        member = mate_from(i)[1]
        return remote(part.at[0, at], team.at[member, at], ps.at[g, i], pr.at[g, i], other)

    def give_all(g):
        def send(i, _):
            @pl.when(mate(i)[0] < 3)
            def _():
                give(i, g).start()

            return 0

        lax.fori_loop(1, TEAM, send, 0)

    def wait_asked(g):
        def wait(i, _):
            asked(i, g).wait_recv()
            return 0

        lax.fori_loop(1, TEAM, wait, 0)

    def one_tile(t, _):
        for g, (t0, _count) in enumerate(parts):
            pl.when(t == t0)(functools.partial(wait_asked, g))

        def rows(k):
            pieces = []
            for e in range(EIGHTHS):
                pairs_of = [named[q * EIGHTHS + e, t, 2 * k : 2 * k + 2, :] for q in range(N_X)]
                pieces.append(jnp.concatenate(pairs_of, 0))
            return jnp.concatenate(pieces, 1)

        v1, s1, v2, s2 = tile_rates(rows(0), rows(1), 128)
        for k, v, st in ((0, v1, s1), (1, v2, s2)):
            full = jnp.concatenate([v, st], 0)
            for q in range(3):
                for e in range(EIGHTHS):
                    piece = full[2 * q : 2 * q + 2, LANES * e : LANES * (e + 1)]
                    part[q * EIGHTHS + e, t, 2 * k : 2 * k + 2, :] = piece
        for g, (t0, count) in enumerate(lots):
            pl.when(t == t0 + count - 1)(functools.partial(give_all, g))
        return 0

    lax.fori_loop(0, TILES_DEV, one_tile, 0)

    @pl.when(active)
    def _():
        team[me] = part[me]
        r = lax.broadcasted_iota(jnp.int32, (8 * N_Z * 8, 1), 0)
        key = ((r // 8) * BLK_DEV + r % 4) * 2 + (r % 8) // 4
        pick[...] = jnp.where(key == keys_ref[...], 1.0, 0.0).astype(bf16)

        def wait(i, _):
            for g in range(2):
                given(i, g).wait_recv()
            return 0

        lax.fori_loop(1, TEAM, wait, 0)
        terms = jnp.concatenate(split3(team[...].reshape(TEAM * TILES_DEV * 4, LANES)), 1)
        sums = lax.dot_general(pick[...], terms, NN, preferred_element_type=f32)
        sums = sums[:, 0:LANES] + (sums[:, LANES : 2 * LANES] + sums[:, 2 * LANES :])
        dense[...] = sums.reshape(N_Z, 8, 8, LANES)
        for i, dz in enumerate(Z_OFFSETS):
            there = dense.at[wrap(z + dz, N_Z)]
            remote(there, zin.at[i], zs.at[i], zr.at[i], along_z(dz)).start()
        for i in range(7):
            remote(dense.at[0], zin.at[i], zs.at[i], zr.at[i], other).wait_recv()
        total = dense[z]
        for i in range(7):
            total = total + zin[i]
        dense[z] = total
        fin[me] = dense[z, x * 2 + core]

        def send(i, _):
            _, _, column, to = mate(i)
            remote(dense.at[z, column], fin.at[me], fs.at[i], fr.at[i], to).start()
            return 0

        lax.fori_loop(1, TEAM, send, 0)

    def settle(i, _):
        for g in range(2):
            ask(i, g).wait_send()

        @pl.when(mate(i)[0] < 3)
        def _():
            for g in range(2):
                give(i, g).wait_send()

        return 0

    lax.fori_loop(1, TEAM, settle, 0)
    for copy in sends:
        copy.wait_send()

    def last(i, _):
        from_x, member = mate_from(i)

        @pl.when(from_x < 3)
        def _():
            remote(dense.at[0, 0], fin.at[member], fs.at[i], fr.at[i], other).wait_recv()

        @pl.when(active)
        def _():
            _, _, column, to = mate(i)
            remote(dense.at[z, column], fin.at[me], fs.at[i], fr.at[i], to).wait_send()

        return 0

    lax.fori_loop(1, TEAM, last, 0)

    @pl.when(active)
    def _():
        for i, dz in enumerate(Z_OFFSETS):
            there = dense.at[wrap(z + dz, N_Z)]
            remote(there, zin.at[i], zs.at[i], zr.at[i], along_z(dz)).wait_send()

    outs = [(vel_out, 0), (vel_out, 1), (vel_out, 2), (str_out, 0), (str_out, 1), (str_out, 2)]
    for q in range(3):
        for e in range(EIGHTHS):
            full = fin[q * EIGHTHS + e]
            for c in range(2):
                ref, row = outs[2 * q + c]
                for b in range(BLK_DEV):
                    at = slice(b * BS + e * LANES, b * BS + (e + 1) * LANES)
                    ref[row : row + 1, at] = full[c * 4 + b : c * 4 + b + 1]


def run(ids, keys, positions, strengths, radii):
    vmem, smem = pl.BlockSpec(memory_space=pltpu.VMEM), pl.BlockSpec(memory_space=pltpu.SMEM)
    dma = pltpu.SemaphoreType.DMA
    out = jax.ShapeDtypeStruct((3, BLK_DEV * BS), f32)
    buffers = [
        (N_X, N_CORE, BLK_DEV, 2, LANES),
        (NB, 2, LANES),
        (TEAM, TILES_DEV, 4, LANES),
        (TEAM, TILES_DEV, 4, LANES),
        (SENDERS, TILES_DEV, 4, LANES),
        (TEAM, TILES_DEV, 4, LANES),
    ]
    late = [(N_Z, 8, 8, LANES), (7, 8, 8, LANES), (SENDERS, 8, LANES)]
    counts = [(7,), (7,), (2, TEAM), (2, TEAM), (7,), (TEAM,)]
    return pl.pallas_call(
        kernel,
        out_shape=(out, out),
        in_specs=[smem, vmem, vmem, vmem, vmem],
        out_specs=(vmem, vmem),
        scratch_shapes=[pltpu.VMEM(b, f32) for b in buffers]
        + [pltpu.VMEM((8 * N_Z * 8, TEAM * TILES_DEV * 4), bf16)]
        + [pltpu.VMEM(b, f32) for b in late]
        + [dma(c) for c in counts for _ in range(2)],
        compiler_params=pltpu.CompilerParams(
            collective_id=0, has_side_effects=True, vmem_limit_bytes=48 * 2**20
        ),
    )(ids, keys, positions, strengths, radii)


def body(positions, strengths, core_radii, tile_pairs, block_home):
    z = lax.axis_index("gx") // (2 * N_X)
    teams = tile_pairs.reshape(N_Z, TEAM * SLOTS)
    logical = lax.dynamic_index_in_dim(teams, z, 0, keepdims=False)
    blocks = jnp.arange(NB, dtype=jnp.int32)
    stored = jnp.sum(jnp.where(logical[:, None] == blocks, block_home, 0), axis=1)
    keys = (stored[:, None] * 2 + jnp.arange(2, dtype=jnp.int32)).reshape(1, -1)
    return run(stored, keys, positions, strengths, core_radii[None, :])


def solution(mesh):
    return jax.shard_map(
        body,
        mesh=mesh,
        in_specs=(P(None, "gx"), P(None, "gx"), P("gx"), P(), P()),
        out_specs=(P(None, "gx"), P(None, "gx")),
        check_vma=False,
    )
```

```python
import functools

import jax
import jax.numpy as jnp
from jax import lax
from jax.experimental import pallas as pl
from jax.experimental.pallas import tpu as pltpu
from jax.sharding import PartitionSpec as P

BS = 1024
TILES_DEV = 8
BLK_DEV = 4
N_Z, N_X, N_CORE, N_Y = 8, 4, 2, 4
N_J = N_X * N_CORE
TEAM = N_Z * N_Y
SLOTS = 2 * TILES_DEV
NB = 256
ROW = BLK_DEV * N_Z
EARLY = TILES_DEV - 1
LANES = 128
MESH = pl.DeviceIdType.MESH

inv_four_pi = 0.07957747154594767
f32, bf16 = jnp.float32, jnp.bfloat16
NT = (((1,), (1,)), ((), ()))
NN = (((1,), (0,)), ((), ()))


def split3(a):
    hi = a.astype(bf16)
    rest = a - hi.astype(f32)
    mid = rest.astype(bf16)
    lo = (rest - mid.astype(f32)).astype(bf16)
    return hi, mid, lo


def split2(v):
    hi = v.astype(bf16)
    return hi, (v - hi.astype(f32)).astype(bf16)


def cross_rows(a, b):
    a0, a1, a2 = (a[k : k + 1] for k in range(3))
    b0, b1, b2 = (b[k : k + 1] for k in range(3))
    return jnp.concatenate([a1 * b2 - a2 * b1, a2 * b0 - a0 * b2, a0 * b1 - a1 * b0], 0)


def moments(x, w):
    base = jnp.concatenate([w, cross_rows(x, w), jnp.zeros((2, w.shape[1]), f32)], 0)
    parts = [base] + [x[k : k + 1] * base for k in range(3)]
    full = split3(jnp.concatenate(parts, 0))
    return jnp.concatenate([s[:8] for s in full], 0), jnp.concatenate(full, 0)


def gains(x, w, a, s):
    a = a[0:8] + (a[8:16] + a[16:24])
    s = s[0:32] + (s[32:64] + s[64:96])
    along = x[0:1] * w[0:1] + x[1:2] * w[1:2] + x[2:3] * w[2:3]
    t = along * s[0:8] - (w[0:1] * s[8:16] + w[1:2] * s[16:24] + w[2:3] * s[24:32])
    vel = (cross_rows(x, a[0:3]) - a[3:6]) * -inv_four_pi
    turn = cross_rows(x, t[0:3]) - t[3:6]
    stretch = (3.0 * inv_four_pi) * turn - inv_four_pi * cross_rows(w, a[0:3])
    return vel, stretch


def tile_rates(first, second, piece):
    n = first.shape[1]
    total = jnp.sum(first[0:3], axis=1, keepdims=True) + jnp.sum(second[0:3], axis=1, keepdims=True)
    centre = total * (0.5 / n)
    xp, xq = first[0:3] - centre, second[0:3] - centre
    wp, wq = first[3:6], second[3:6]
    sp, sq = 0.5 * first[6:7] * first[6:7], 0.5 * second[6:7] * second[6:7]
    bp, mp = moments(xp, wp)
    bq, mq = moments(xq, wq)
    cols = jnp.transpose(jnp.concatenate([first[0:3], sp, first[4:8]], 0))
    aq = jnp.zeros((24, n), f32)
    hq = jnp.zeros((96, n), f32)
    ap, hp = [], []
    dot = functools.partial(lax.dot_general, preferred_element_type=f32)
    for s in range(0, n, piece):
        cs = cols[s : s + piece]
        r = [cs[:, k : k + 1] - second[k : k + 1] for k in range(3)]
        g = r[0] * r[0] + r[1] * r[1] + r[2] * r[2] + (cs[:, 3:4] + sq)
        q = lax.rsqrt(g)
        q2 = q * q
        f = q2 * q
        h = f * q2
        fh, fl = split2(f)
        hh, hl = split2(h)
        ap.append(dot(fh, bq, NT) + dot(fl, bq, NT))
        hp.append(dot(hh, mq, NT) + dot(hl, mq, NT))
        bps, mps = bp[:, s : s + piece], mp[:, s : s + piece]
        aq = aq + (dot(bps, fh, NN) + dot(bps, fl, NN))
        hq = hq + (dot(mps, hh, NN) + dot(mps, hl, NN))
    ap, hp = jnp.transpose(jnp.concatenate(ap, 0)), jnp.transpose(jnp.concatenate(hp, 0))
    return gains(xp, wp, ap, hp) + gains(xq, wq, aq, hq)


def place():
    gx, y = lax.axis_index("gx"), lax.axis_index("gy")
    return gx // N_J, lax.rem(gx, N_J), y


def wrap(v, n):
    return lax.rem(v + n, n)


J_STEPS = [(2, 0), (2, 1), (1, 0), (3, 0), (1, 1), (3, 1), (0, 1)]
Z_STEPS = [4, 3, 5, 2, 6, 1, 7]


def remote(src, dst, send, recv, device):
    return pltpu.make_async_remote_copy(
        src_ref=src, dst_ref=dst, send_sem=send, recv_sem=recv, device_id=device, device_id_type=MESH
    )


def iota(shape, axis):
    return lax.broadcasted_iota(jnp.int32, shape, axis)


def dot32(a, b):
    return lax.dot_general(a, b, NN, preferred_element_type=f32)


def kernel(
    pairs_ref, home_ref, pairs_vec, home_vec, pos_ref, str_ref, rad_ref, vel_out, str_out,
    mix, own, grid, pack, named, part, team, final_team, dense, jin, fin, pick, final_pick,
    os, orr, gs, gr, ts, tr, ps, pr, js, jr, fs, fr,
):
    z, j, y = place()
    x, core = j // 2, lax.rem(j, 2)
    gx = z * N_J + j
    me = z * N_Y + y
    other = (gx, wrap(y + 1, N_Y))
    active = y < 3

    def mate(i):
        tz, ty = wrap(z + i // N_Y, N_Z), wrap(y + i % N_Y, N_Y)
        return tz, ty, tz * N_Y + ty, (tz * N_J + j, ty)

    def mate_from(i):
        tz, ty = wrap(z - i // N_Y, N_Z), wrap(y - i % N_Y, N_Y)
        return ty, tz * N_Y + ty

    def near(step, way=1):
        dx, dc = step
        return wrap(x + way * dx, N_X) * 2 + lax.rem(core + dc, 2)

    barrier = pltpu.get_barrier_semaphore()
    for i in list(range(1, TEAM)):
        pl.semaphore_signal(barrier, inc=1, device_id=mate(i)[3], device_id_type=MESH)
    for step in J_STEPS:
        to = (z * N_J + near(step), y)
        pl.semaphore_signal(barrier, inc=1, device_id=to, device_id_type=MESH)

    rows_of = [(pos_ref, 0), (pos_ref, 1), (pos_ref, 2), (str_ref, 0), (str_ref, 1), (str_ref, 2)]
    for k, (ref, row) in enumerate(rows_of + [(rad_ref, 0)]):
        mix[k // 2, k % 2 : k % 2 + 1, :] = ref[row : row + 1, :]
    mix[3, 1:2, :] = jnp.zeros((1, BLK_DEV * BS), f32)
    for tz in range(N_Z):
        for b in range(BLK_DEV):
            own[tz, b] = mix[y, :, b * BS + tz * LANES : b * BS + (tz + 1) * LANES]

    def numbers(lanes, row_at):
        chosen = jnp.where(iota((2 * TEAM * TILES_DEV * 4, lanes), 0) == row_at, 1.0, 0.0)
        logical = dot32(pairs_vec[...].astype(f32).astype(bf16), chosen.astype(bf16))
        home = jnp.broadcast_to(home_vec[...], (8, NB)).astype(f32).astype(bf16)
        stored = []
        for k in range(2):
            match = jnp.where(iota((NB, lanes), 0).astype(f32) == logical[k : k + 1], 1.0, 0.0)
            stored.append(dot32(home, match.astype(bf16))[0:1])
        return stored

    r = iota((8 * N_J * N_Z, 1), 0)
    row_key = (((r // 8) * BLK_DEV + r % 4) * 2 + (r % 8) // 4).astype(f32)

    def one_hot(key):
        return jnp.where(row_key == key, 1.0, 0.0).astype(bf16)

    lanes = TEAM * TILES_DEV
    k = iota((1, lanes), 1)
    stored = numbers(lanes, ((k // 32) * N_J + j) * 32 + k % 32)
    for kc in range(4):
        pick[:, lanes * kc : lanes * (kc + 1)] = one_hot(stored[kc // 2] * 2.0 + kc % 2)
    k = iota((1, 4 * TEAM), 1)
    m = k % TEAM
    stored = numbers(4 * TEAM, ((m // N_Y) * N_J + j) * 32 + (m % N_Y) * TILES_DEV + TILES_DEV - 1)
    key = jnp.where(k < 2 * TEAM, stored[0], stored[1]) * 2.0 + ((k // TEAM) % 2).astype(f32)
    final_pick[...] = one_hot(key)
    for m in range(TEAM):
        team[m, TILES_DEV - 1] = jnp.zeros((4, LANES), f32)
    pl.semaphore_wait(barrier, TEAM - 1 + len(J_STEPS))

    def home_of(tj, tz):
        return grid.at[pl.ds(tj * ROW + tz * BLK_DEV, BLK_DEV)]

    def row_of(tj):
        return grid.at[pl.ds(tj * ROW, ROW)]

    sends = []
    for i, dz in enumerate(Z_STEPS):
        tz = wrap(z + dz, N_Z)
        copy = remote(own.at[tz], home_of(j, z), os.at[i], orr.at[i], (tz * N_J + j, y))
        copy.start()
        sends.append(copy)
    for b in range(BLK_DEV):
        grid[j * ROW + z * BLK_DEV + b] = own[z, b]
    for i, dz in enumerate(Z_STEPS):
        there = home_of(j, wrap(z - dz, N_Z))
        remote(own.at[0], there, os.at[i], orr.at[i], other).wait_recv()
    for i, step in enumerate(J_STEPS):
        copy = remote(row_of(j), row_of(j), gs.at[i], gr.at[i], (z * N_J + near(step), y))
        copy.start()
        sends.append(copy)
    for i, step in enumerate(J_STEPS):
        row = row_of(near(step, -1))
        remote(row, row, gs.at[i], gr.at[i], other).wait_recv()

    parts = ((0, 1), (1, EARLY))

    def block_of(tz, ty, t, k):
        row = (tz * N_J + j) * 32 + ty * TILES_DEV + t
        return home_ref[pairs_ref[k * 2 * TEAM * TILES_DEV * 4 + row]]

    def ask(i, g):
        at = pl.ds(*parts[g])
        return remote(pack.at[i, at], named.at[me, at], ts.at[g, i], tr.at[g, i], mate(i)[3])

    def asked(i, g):
        at = pl.ds(*parts[g])
        member = mate_from(i)[1]
        return remote(pack.at[i, at], named.at[member, at], ts.at[g, i], tr.at[g, i], other)

    for g, (t0, count) in enumerate(parts):

        def send(i, _, g=g, t0=t0, count=count):
            tz, ty, _, _ = mate(i)
            for t in range(t0, t0 + count):
                for k in range(2):
                    pack[i, t, 2 * k : 2 * k + 2, :] = grid[block_of(tz, ty, t, k)]
            ask(i, g).start()
            return 0

        lax.fori_loop(1, TEAM, send, 0)
    for t in range(TILES_DEV):
        for k in range(2):
            named[me, t, 2 * k : 2 * k + 2, :] = grid[block_of(z, y, t, k)]

    lots = ((0, EARLY), (EARLY, 1))

    def give(i, g):
        at = pl.ds(*lots[g])
        _, _, member, to = mate(i)
        there = team.at[me, at] if g == 0 else final_team.at[pl.ds(me, 1)]
        return remote(part.at[member, at], there, ps.at[g, i], pr.at[g, i], to)

    def given(i, g):
        at = pl.ds(*lots[g])
        member = mate_from(i)[1]
        here = team.at[member, at] if g == 0 else final_team.at[pl.ds(member, 1)]
        return remote(part.at[0, at], here, ps.at[g, i], pr.at[g, i], other)

    def give_all(g):
        def send(i, _):
            @pl.when(mate(i)[1] < 3)
            def _():
                give(i, g).start()

            return 0

        lax.fori_loop(1, TEAM, send, 0)

    def wait_asked(g):
        def wait(i, _):
            asked(i, g).wait_recv()
            return 0

        lax.fori_loop(1, TEAM, wait, 0)

    def one_tile(t, _):
        for g, (t0, _count) in enumerate(parts):
            pl.when(t == t0)(functools.partial(wait_asked, g))

        def rows(k):
            pieces = []
            for e in range(N_Z):
                pairs_of = [named[e * N_Y + q, t, 2 * k : 2 * k + 2, :] for q in range(N_Y)]
                pieces.append(jnp.concatenate(pairs_of, 0))
            return jnp.concatenate(pieces, 1)

        v1, s1, v2, s2 = tile_rates(rows(0), rows(1), 128)
        for k, v, st in ((0, v1, s1), (1, v2, s2)):
            full = jnp.concatenate([v, st], 0)
            for q in range(3):
                for e in range(N_Z):
                    piece = full[2 * q : 2 * q + 2, LANES * e : LANES * (e + 1)]
                    part[e * N_Y + q, t, 2 * k : 2 * k + 2, :] = piece
        for g, (t0, count) in enumerate(lots):
            pl.when(t == t0 + count - 1)(functools.partial(give_all, g))
        return 0

    lax.fori_loop(0, TILES_DEV, one_tile, 0)

    def by_block(chosen, terms):
        sums = dot32(chosen, jnp.concatenate(split3(terms), 1))
        return sums[:, 0:LANES] + (sums[:, LANES : 2 * LANES] + sums[:, 2 * LANES :])

    @pl.when(active)
    def _():
        team[me, 0:EARLY] = part[me, 0:EARLY]
        final_team[me] = part[me, EARLY]

        def wait(g, i, _):
            given(i, g).wait_recv()
            return 0

        lax.fori_loop(1, TEAM, functools.partial(wait, 0), 0)
        lanes = TEAM * TILES_DEV
        terms = jnp.concatenate([team[:, :, kc, :].reshape(lanes, LANES) for kc in range(4)], 0)
        sums = by_block(pick[...], terms)
        lax.fori_loop(1, TEAM, functools.partial(wait, 1), 0)
        terms = jnp.concatenate([final_team[:, kc, :] for kc in range(4)], 0)
        sums = sums + by_block(final_pick[...], terms)
        dense[...] = sums.reshape(N_J, N_Z, 8, LANES)
        for i, step in enumerate(J_STEPS):
            tj = near(step)
            remote(dense.at[tj], jin.at[i], js.at[i], jr.at[i], (z * N_J + tj, y)).start()
        for i in range(7):
            remote(dense.at[0], jin.at[i], js.at[i], jr.at[i], other).wait_recv()
        total = dense[j]
        for i in range(7):
            total = total + jin[i]
        dense[j] = total
        fin[me] = dense[j, z]

        def send(i, _):
            tz, _, _, to = mate(i)
            remote(dense.at[j, tz], fin.at[me], fs.at[i], fr.at[i], to).start()
            return 0

        lax.fori_loop(1, TEAM, send, 0)

    def settle(i, _):
        for g in range(2):
            ask(i, g).wait_send()

        @pl.when(mate(i)[1] < 3)
        def _():
            for g in range(2):
                give(i, g).wait_send()

        return 0

    lax.fori_loop(1, TEAM, settle, 0)
    for copy in sends:
        copy.wait_send()

    @pl.when(active)
    def _():
        for i, step in enumerate(J_STEPS):
            remote(dense.at[near(step)], jin.at[i], js.at[i], jr.at[i], other).wait_send()

    def last(i, _):
        from_y, member = mate_from(i)

        @pl.when(from_y < 3)
        def _():
            remote(dense.at[0, 0], fin.at[member], fs.at[i], fr.at[i], other).wait_recv()

        @pl.when(active)
        def _():
            tz, _, _, to = mate(i)
            remote(dense.at[j, tz], fin.at[me], fs.at[i], fr.at[i], to).wait_send()

        return 0

    lax.fori_loop(1, TEAM, last, 0)
    outs = [(vel_out, 0), (vel_out, 1), (vel_out, 2), (str_out, 0), (str_out, 1), (str_out, 2)]
    for q in range(3):
        for e in range(N_Z):
            full = fin[e * N_Y + q]
            for c in range(2):
                ref, row = outs[2 * q + c]
                for b in range(BLK_DEV):
                    at = slice(b * BS + e * LANES, b * BS + (e + 1) * LANES)
                    ref[row : row + 1, at] = full[c * 4 + b : c * 4 + b + 1]


def run(pairs, home, positions, strengths, radii):
    vmem, smem = pl.BlockSpec(memory_space=pltpu.VMEM), pl.BlockSpec(memory_space=pltpu.SMEM)
    dma = pltpu.SemaphoreType.DMA
    out = jax.ShapeDtypeStruct((3, BLK_DEV * BS), f32)
    buffers = [
        (N_Y, 2, BLK_DEV * BS),
        (N_Z, BLK_DEV, 2, LANES),
        (NB, 2, LANES),
        (TEAM, TILES_DEV, 4, LANES),
        (TEAM, TILES_DEV, 4, LANES),
        (TEAM, TILES_DEV, 4, LANES),
        (TEAM, TILES_DEV, 4, LANES),
        (TEAM, 4, LANES),
        (N_J, N_Z, 8, LANES),
        (7, N_Z, 8, LANES),
        (TEAM, 8, LANES),
    ]
    chosen = [(8 * N_J * N_Z, 4 * TEAM * TILES_DEV), (8 * N_J * N_Z, 4 * TEAM)]
    counts = [(7,), (7,), (2, TEAM), (2, TEAM), (7,), (TEAM,)]
    return pl.pallas_call(
        kernel,
        out_shape=(out, out),
        in_specs=[smem, smem, vmem, vmem, vmem, vmem, vmem],
        out_specs=(vmem, vmem),
        scratch_shapes=[pltpu.VMEM(b, f32) for b in buffers]
        + [pltpu.VMEM(b, bf16) for b in chosen]
        + [dma(c) for c in counts for _ in range(2)],
        compiler_params=pltpu.CompilerParams(
            collective_id=0, has_side_effects=True, vmem_limit_bytes=48 * 2**20
        ),
    )(pairs.reshape(-1), home, pairs, home[None, :], positions, strengths, radii)


def body(positions, strengths, core_radii, tile_pairs, block_home):
    gx, b = block_home // BLK_DEV, block_home % BLK_DEV
    home = ((gx % N_J) * N_Z + gx // N_J) * BLK_DEV + b
    return run(tile_pairs.T, home, positions, strengths, core_radii[None, :])


def solution(mesh):
    return jax.shard_map(
        body,
        mesh=mesh,
        in_specs=(P(None, "gx"), P(None, "gx"), P("gx"), P(), P()),
        out_specs=(P(None, "gx"), P(None, "gx")),
        check_vma=False,
    )
```

```python
import functools

import jax
import jax.numpy as jnp
from jax import lax
from jax.experimental import pallas as pl
from jax.experimental.pallas import tpu as pltpu
from jax.sharding import PartitionSpec as P

BS = 1024
TILES_DEV = 8
BLK_DEV = 4
N_Z, N_X, N_CORE, N_Y = 8, 4, 2, 4
N_J = N_X * N_CORE
TEAM = N_Z * N_Y
SLOTS = 2 * TILES_DEV
NB = 256
ROW = BLK_DEV * N_Z
EARLY = TILES_DEV - 1
LANES = 128
MESH = pl.DeviceIdType.MESH

inv_four_pi = 0.07957747154594767
f32, bf16 = jnp.float32, jnp.bfloat16
NT = (((1,), (1,)), ((), ()))
NN = (((1,), (0,)), ((), ()))


def split3(a):
    hi = a.astype(bf16)
    rest = a - hi.astype(f32)
    mid = rest.astype(bf16)
    lo = (rest - mid.astype(f32)).astype(bf16)
    return hi, mid, lo


def split2(v):
    hi = v.astype(bf16)
    return hi, (v - hi.astype(f32)).astype(bf16)


def cross_rows(a, b):
    a0, a1, a2 = (a[k : k + 1] for k in range(3))
    b0, b1, b2 = (b[k : k + 1] for k in range(3))
    return jnp.concatenate([a1 * b2 - a2 * b1, a2 * b0 - a0 * b2, a0 * b1 - a1 * b0], 0)


def moments(x, w):
    base = jnp.concatenate([w, cross_rows(x, w), jnp.zeros((2, w.shape[1]), f32)], 0)
    parts = [base] + [x[k : k + 1] * base for k in range(3)]
    full = split3(jnp.concatenate(parts, 0))
    return jnp.concatenate([s[:8] for s in full], 0), jnp.concatenate(full, 0)


def gains(x, w, a, s):
    a = a[0:8] + (a[8:16] + a[16:24])
    s = s[0:32] + (s[32:64] + s[64:96])
    along = x[0:1] * w[0:1] + x[1:2] * w[1:2] + x[2:3] * w[2:3]
    t = along * s[0:8] - (w[0:1] * s[8:16] + w[1:2] * s[16:24] + w[2:3] * s[24:32])
    vel = (cross_rows(x, a[0:3]) - a[3:6]) * -inv_four_pi
    turn = cross_rows(x, t[0:3]) - t[3:6]
    stretch = (3.0 * inv_four_pi) * turn - inv_four_pi * cross_rows(w, a[0:3])
    return vel, stretch


def tile_rates(first, second, piece):
    n = first.shape[1]
    total = jnp.sum(first[0:3], axis=1, keepdims=True) + jnp.sum(second[0:3], axis=1, keepdims=True)
    centre = total * (0.5 / n)
    xp, xq = first[0:3] - centre, second[0:3] - centre
    wp, wq = first[3:6], second[3:6]
    sp, sq = 0.5 * first[6:7] * first[6:7], 0.5 * second[6:7] * second[6:7]
    bp, mp = moments(xp, wp)
    bq, mq = moments(xq, wq)
    cols = jnp.transpose(jnp.concatenate([first[0:3], sp, first[4:8]], 0))
    aq = jnp.zeros((24, n), f32)
    hq = jnp.zeros((96, n), f32)
    ap, hp = [], []
    dot = functools.partial(lax.dot_general, preferred_element_type=f32)
    for s in range(0, n, piece):
        cs = cols[s : s + piece]
        r = [cs[:, k : k + 1] - second[k : k + 1] for k in range(3)]
        g = r[0] * r[0] + r[1] * r[1] + r[2] * r[2] + (cs[:, 3:4] + sq)
        q = lax.rsqrt(g)
        q2 = q * q
        f = q2 * q
        h = f * q2
        fh, fl = split2(f)
        hh, hl = split2(h)
        ap.append(dot(fh, bq, NT) + dot(fl, bq, NT))
        hp.append(dot(hh, mq, NT) + dot(hl, mq, NT))
        bps, mps = bp[:, s : s + piece], mp[:, s : s + piece]
        aq = aq + (dot(bps, fh, NN) + dot(bps, fl, NN))
        hq = hq + (dot(mps, hh, NN) + dot(mps, hl, NN))
    ap, hp = jnp.transpose(jnp.concatenate(ap, 0)), jnp.transpose(jnp.concatenate(hp, 0))
    return gains(xp, wp, ap, hp) + gains(xq, wq, aq, hq)


def place():
    gx, y = lax.axis_index("gx"), lax.axis_index("gy")
    return gx // N_J, lax.rem(gx, N_J), y


def wrap(v, n):
    return lax.rem(v + n, n)


J_STEPS = [(2, 0), (2, 1), (1, 0), (3, 0), (1, 1), (3, 1), (0, 1)]
Z_STEPS = [4, 3, 5, 2, 6, 1, 7]


def remote(src, dst, send, recv, device):
    return pltpu.make_async_remote_copy(
        src_ref=src, dst_ref=dst, send_sem=send, recv_sem=recv, device_id=device, device_id_type=MESH
    )


def number_of(storage):
    z, j = lax.shift_right_logical(storage, 5), lax.shift_right_logical(storage, 2) & (N_J - 1)
    return j * ROW + z * BLK_DEV + (storage & (BLK_DEV - 1))


def iota(shape, axis):
    return lax.broadcasted_iota(jnp.int32, shape, axis)


def dot32(a, b):
    return lax.dot_general(a, b, NN, preferred_element_type=f32)


def kernel(
    pairs_ref, home_ref, pairs_hbm, home_hbm, pos_hbm, str_hbm, rad_hbm, vel_out, str_out,
    table, pairs_vec, home_vec, pos_ref, str_ref, rad_ref, mix, own, grid, pack, named, part, team, final_team, dense, jin, fin, pick, final_pick,
    loads, os, orr, gs, gr, ts, tr, ps, pr, js, jr, fs, fr,
):
    z, j, y = place()
    x, core = j // 2, lax.rem(j, 2)
    gx = z * N_J + j
    me = z * N_Y + y
    other = (gx, wrap(y + 1, N_Y))
    active = y < 3

    def mate(i):
        tz, ty = wrap(z + i // N_Y, N_Z), wrap(y + i % N_Y, N_Y)
        return tz, ty, tz * N_Y + ty, (tz * N_J + j, ty)

    def mate_from(i):
        tz, ty = wrap(z - i // N_Y, N_Z), wrap(y - i % N_Y, N_Y)
        return ty, tz * N_Y + ty

    def near(step, way=1):
        dx, dc = step
        return wrap(x + way * dx, N_X) * 2 + lax.rem(core + dc, 2)

    incoming = [(pos_hbm, pos_ref), (str_hbm, str_ref), (rad_hbm, rad_ref)]
    incoming += [(pairs_hbm, pairs_vec), (home_hbm, home_vec)]
    incoming = [pltpu.make_async_copy(a, b, loads.at[i]) for i, (a, b) in enumerate(incoming)]
    for copy in incoming:
        copy.start()
    barrier = pltpu.get_barrier_semaphore()
    greeted = [(wrap(z + dz, N_Z) * N_J + j, y) for dz in Z_STEPS]
    greeted += [(gx, wrap(y + dy, N_Y)) for dy in (2, 1, 3)]
    greeted += [(z * N_J + near(step), y) for step in J_STEPS]
    for to in greeted:
        pl.semaphore_signal(barrier, inc=1, device_id=to, device_id_type=MESH)


    def enter(b, _):
        table[b] = number_of(home_ref[b])
        return 0

    lax.fori_loop(0, NB, enter, 0, unroll=8)
    for copy in incoming:
        copy.wait()
    rows_of = [(pos_ref, 0), (pos_ref, 1), (pos_ref, 2), (str_ref, 0), (str_ref, 1), (str_ref, 2)]
    for k, (ref, row) in enumerate(rows_of + [(rad_ref, 0)]):
        mix[k // 2, k % 2 : k % 2 + 1, :] = ref[row : row + 1, :]
    mix[3, 1:2, :] = jnp.zeros((1, BLK_DEV * BS), f32)
    for tz in range(N_Z):
        for b in range(BLK_DEV):
            own[tz, b] = mix[y, :, b * BS + tz * LANES : b * BS + (tz + 1) * LANES]

    pl.semaphore_wait(barrier, len(greeted))

    def home_of(tj, tz):
        return grid.at[pl.ds(tj * ROW + tz * BLK_DEV, BLK_DEV)]

    def row_of(tj):
        return grid.at[pl.ds(tj * ROW, ROW)]

    sends = []
    for i, dz in enumerate(Z_STEPS):
        tz = wrap(z + dz, N_Z)
        copy = remote(own.at[tz], home_of(j, z), os.at[i], orr.at[i], (tz * N_J + j, y))
        copy.start()
        sends.append(copy)
    for b in range(BLK_DEV):
        grid[j * ROW + z * BLK_DEV + b] = own[z, b]
    for i, dz in enumerate(Z_STEPS):
        there = home_of(j, wrap(z - dz, N_Z))
        remote(own.at[0], there, os.at[i], orr.at[i], other).wait_recv()
    for i, step in enumerate(J_STEPS):
        copy = remote(row_of(j), row_of(j), gs.at[i], gr.at[i], (z * N_J + near(step), y))
        copy.start()
        sends.append(copy)
    def numbers(lanes, row_at):
        chosen = jnp.where(iota((2 * TEAM * TILES_DEV * 4, lanes), 0) == row_at, 1.0, 0.0)
        logical = dot32(pairs_vec[...].astype(f32).astype(bf16), chosen.astype(bf16))
        home = jnp.broadcast_to(number_of(home_vec[...]), (8, NB)).astype(f32).astype(bf16)
        stored = []
        for k in range(2):
            match = jnp.where(iota((NB, lanes), 0).astype(f32) == logical[k : k + 1], 1.0, 0.0)
            stored.append(dot32(home, match.astype(bf16))[0:1])
        return stored

    r = iota((8 * N_J * N_Z, 1), 0)
    row_key = (((r // 8) * BLK_DEV + r % 4) * 2 + (r % 8) // 4).astype(f32)

    def one_hot(key):
        return jnp.where(row_key == key, 1.0, 0.0).astype(bf16)

    lanes = TEAM * TILES_DEV
    k = iota((1, lanes), 1)
    stored = numbers(lanes, ((k // 32) * N_J + j) * 32 + k % 32)
    for kc in range(4):
        pick[:, lanes * kc : lanes * (kc + 1)] = one_hot(stored[kc // 2] * 2.0 + kc % 2)
    k = iota((1, 4 * TEAM), 1)
    m = k % TEAM
    stored = numbers(4 * TEAM, ((m // N_Y) * N_J + j) * 32 + (m % N_Y) * TILES_DEV + TILES_DEV - 1)
    key = jnp.where(k < 2 * TEAM, stored[0], stored[1]) * 2.0 + ((k // TEAM) % 2).astype(f32)
    final_pick[...] = one_hot(key)
    for m in range(TEAM):
        team[m, TILES_DEV - 1] = jnp.zeros((4, LANES), f32)
    for i, step in enumerate(J_STEPS):
        row = row_of(near(step, -1))
        remote(row, row, gs.at[i], gr.at[i], other).wait_recv()

    parts = ((0, 1), (1, 2), (3, TILES_DEV - 3))

    def block_of(tz, ty, t, k):
        row = (tz * N_J + j) * 32 + ty * TILES_DEV + t
        return table[pairs_ref[k, row]]

    def ask(i, g):
        at = pl.ds(*parts[g])
        return remote(pack.at[i, at], named.at[me, at], ts.at[g, i], tr.at[g, i], mate(i)[3])

    def asked(i, g):
        at = pl.ds(*parts[g])
        member = mate_from(i)[1]
        return remote(pack.at[i, at], named.at[member, at], ts.at[g, i], tr.at[g, i], other)

    for g, (t0, count) in enumerate(parts):

        def send(i, _, g=g, t0=t0, count=count):
            tz, ty, _, _ = mate(i)
            for t in range(t0, t0 + count):
                for k in range(2):
                    pack[i, t, 2 * k : 2 * k + 2, :] = grid[block_of(tz, ty, t, k)]
            ask(i, g).start()
            return 0

        if g == 0:
            for i in range(1, TEAM):
                send(i, 0)
        else:
            lax.fori_loop(1, TEAM, send, 0)
    for t in range(TILES_DEV):
        for k in range(2):
            named[me, t, 2 * k : 2 * k + 2, :] = grid[block_of(z, y, t, k)]

    lots = ((0, 4), (4, EARLY - 4), (EARLY, 1))

    def give(i, g):
        at = pl.ds(*lots[g])
        _, _, member, to = mate(i)
        there = team.at[me, at] if g < 2 else final_team.at[pl.ds(me, 1)]
        return remote(part.at[member, at], there, ps.at[g, i], pr.at[g, i], to)

    def given(i, g):
        at = pl.ds(*lots[g])
        member = mate_from(i)[1]
        here = team.at[member, at] if g < 2 else final_team.at[pl.ds(member, 1)]
        return remote(part.at[0, at], here, ps.at[g, i], pr.at[g, i], other)

    def give_all(g):
        def send(i, _):
            @pl.when(mate(i)[1] < 3)
            def _():
                give(i, g).start()

            return 0

        if g == 2:
            for i in range(1, TEAM):
                send(i, 0)
        else:
            lax.fori_loop(1, TEAM, send, 0)

    def wait_asked(g):
        def wait(i, _):
            asked(i, g).wait_recv()
            return 0

        lax.fori_loop(1, TEAM, wait, 0)

    def one_tile(t, _):
        for g, (t0, _count) in enumerate(parts):
            pl.when(t == t0)(functools.partial(wait_asked, g))

        def rows(k):
            pieces = []
            for e in range(N_Z):
                pairs_of = [named[e * N_Y + q, t, 2 * k : 2 * k + 2, :] for q in range(N_Y)]
                pieces.append(jnp.concatenate(pairs_of, 0))
            return jnp.concatenate(pieces, 1)

        v1, s1, v2, s2 = tile_rates(rows(0), rows(1), 128)
        for k, v, st in ((0, v1, s1), (1, v2, s2)):
            full = jnp.concatenate([v, st], 0)
            for q in range(3):
                for e in range(N_Z):
                    piece = full[2 * q : 2 * q + 2, LANES * e : LANES * (e + 1)]
                    part[e * N_Y + q, t, 2 * k : 2 * k + 2, :] = piece
        for g, (t0, count) in enumerate(lots):
            pl.when(t == t0 + count - 1)(functools.partial(give_all, g))
        return 0

    lax.fori_loop(0, TILES_DEV, one_tile, 0)

    def by_block(chosen, terms):
        sums = dot32(chosen, jnp.concatenate(split3(terms), 1))
        return sums[:, 0:LANES] + (sums[:, LANES : 2 * LANES] + sums[:, 2 * LANES :])

    @pl.when(active)
    def _():
        team[me, 0:EARLY] = part[me, 0:EARLY]
        final_team[me] = part[me, EARLY]

        def wait(g, i, _):
            given(i, g).wait_recv()
            return 0

        lax.fori_loop(1, TEAM, functools.partial(wait, 0), 0)
        lax.fori_loop(1, TEAM, functools.partial(wait, 1), 0)
        lanes = TEAM * TILES_DEV
        terms = jnp.concatenate([team[:, :, kc, :].reshape(lanes, LANES) for kc in range(4)], 0)
        sums = by_block(pick[...], terms)
        lax.fori_loop(1, TEAM, functools.partial(wait, 2), 0)
        terms = jnp.concatenate([final_team[:, kc, :] for kc in range(4)], 0)
        sums = sums + by_block(final_pick[...], terms)
        dense[...] = sums.reshape(N_J, N_Z, 8, LANES)
        for i, step in enumerate(J_STEPS):
            tj = near(step)
            remote(dense.at[tj], jin.at[i], js.at[i], jr.at[i], (z * N_J + tj, y)).start()
        for i in range(7):
            remote(dense.at[0], jin.at[i], js.at[i], jr.at[i], other).wait_recv()
        total = dense[j]
        for i in range(7):
            total = total + jin[i]
        dense[j] = total
        fin[me] = dense[j, z]

        for i in range(1, TEAM):
            tz, _, _, to = mate(i)
            remote(dense.at[j, tz], fin.at[me], fs.at[i], fr.at[i], to).start()

    def settle(i, _):
        for g in range(3):
            ask(i, g).wait_send()

        @pl.when(mate(i)[1] < 3)
        def _():
            for g in range(3):
                give(i, g).wait_send()

        return 0

    lax.fori_loop(1, TEAM, settle, 0)
    for copy in sends:
        copy.wait_send()

    @pl.when(active)
    def _():
        for i, step in enumerate(J_STEPS):
            remote(dense.at[near(step)], jin.at[i], js.at[i], jr.at[i], other).wait_send()

    def last(i, _):
        from_y, member = mate_from(i)

        @pl.when(from_y < 3)
        def _():
            remote(dense.at[0, 0], fin.at[member], fs.at[i], fr.at[i], other).wait_recv()

        @pl.when(active)
        def _():
            tz, _, _, to = mate(i)
            remote(dense.at[j, tz], fin.at[me], fs.at[i], fr.at[i], to).wait_send()

        return 0

    lax.fori_loop(1, TEAM, last, 0)
    outs = [(vel_out, 0), (vel_out, 1), (vel_out, 2), (str_out, 0), (str_out, 1), (str_out, 2)]
    for q in range(3):
        for e in range(N_Z):
            full = fin[e * N_Y + q]
            for c in range(2):
                ref, row = outs[2 * q + c]
                for b in range(BLK_DEV):
                    at = slice(b * BS + e * LANES, b * BS + (e + 1) * LANES)
                    ref[row : row + 1, at] = full[c * 4 + b : c * 4 + b + 1]


def run(pairs, home, positions, strengths, radii):
    vmem, smem = pl.BlockSpec(memory_space=pltpu.VMEM), pl.BlockSpec(memory_space=pltpu.SMEM)
    dma = pltpu.SemaphoreType.DMA
    out = jax.ShapeDtypeStruct((3, BLK_DEV * BS), f32)
    n = BLK_DEV * BS
    words = [(2, 2 * TEAM * TILES_DEV * 4), (1, NB)]
    buffers = [
        (3, n),
        (3, n),
        (1, n),
        (N_Y, 2, BLK_DEV * BS),
        (N_Z, BLK_DEV, 2, LANES),
        (NB, 2, LANES),
        (TEAM, TILES_DEV, 4, LANES),
        (TEAM, TILES_DEV, 4, LANES),
        (TEAM, TILES_DEV, 4, LANES),
        (TEAM, TILES_DEV, 4, LANES),
        (TEAM, 4, LANES),
        (N_J, N_Z, 8, LANES),
        (7, N_Z, 8, LANES),
        (TEAM, 8, LANES),
    ]
    chosen = [(8 * N_J * N_Z, 4 * TEAM * TILES_DEV), (8 * N_J * N_Z, 4 * TEAM)]
    counts = [(7,), (7,), (3, TEAM), (3, TEAM), (7,), (TEAM,)]
    return pl.pallas_call(
        kernel,
        out_shape=(out, out),
        in_specs=[smem, smem] + [pl.BlockSpec(memory_space=pl.ANY)] * 5,
        out_specs=(vmem, vmem),
        scratch_shapes=[pltpu.SMEM((NB,), jnp.int32)]
        + [pltpu.VMEM(b, jnp.int32) for b in words]
        + [pltpu.VMEM(b, f32) for b in buffers]
        + [pltpu.VMEM(b, bf16) for b in chosen]
        + [dma((5,))]
        + [dma(c) for c in counts for _ in range(2)],
        compiler_params=pltpu.CompilerParams(
            collective_id=0, has_side_effects=True, vmem_limit_bytes=63 * 2**20
        ),
    )(pairs, home, pairs, home[None, :], positions, strengths, radii)


def body(positions, strengths, core_radii, tile_pairs, block_home):
    return run(tile_pairs.T, block_home, positions, strengths, core_radii[None, :])


def solution(mesh):
    return jax.shard_map(
        body,
        mesh=mesh,
        in_specs=(P(None, "gx"), P(None, "gx"), P("gx"), P(), P()),
        out_specs=(P(None, "gx"), P(None, "gx")),
        check_vma=False,
    )
```

```python
import functools

import jax
import jax.numpy as jnp
from jax import lax
from jax.experimental import pallas as pl
from jax.experimental.pallas import tpu as pltpu
from jax.sharding import PartitionSpec as P

BS = 1024
TILES_DEV = 8
BLK_DEV = 4
N_Z, N_X, N_CORE, N_Y = 8, 4, 2, 4
N_J = N_X * N_CORE
TEAM = N_Z * N_Y
SLOTS = 2 * TILES_DEV
NB = 256
ROW = BLK_DEV * N_Z
EARLY = TILES_DEV - 2
LATE = TILES_DEV - EARLY
LANES = 128
MESH = pl.DeviceIdType.MESH

inv_four_pi = 0.07957747154594767
f32, bf16 = jnp.float32, jnp.bfloat16
NT = (((1,), (1,)), ((), ()))
NN = (((1,), (0,)), ((), ()))


def split3(a):
    hi = a.astype(bf16)
    rest = a - hi.astype(f32)
    mid = rest.astype(bf16)
    lo = (rest - mid.astype(f32)).astype(bf16)
    return hi, mid, lo


def split2(v):
    hi = v.astype(bf16)
    return hi, (v - hi.astype(f32)).astype(bf16)


def cross_rows(a, b):
    a0, a1, a2 = (a[k : k + 1] for k in range(3))
    b0, b1, b2 = (b[k : k + 1] for k in range(3))
    return jnp.concatenate([a1 * b2 - a2 * b1, a2 * b0 - a0 * b2, a0 * b1 - a1 * b0], 0)


def moments(x, w):
    base = jnp.concatenate([w, cross_rows(x, w), jnp.zeros((2, w.shape[1]), f32)], 0)
    parts = [base] + [x[k : k + 1] * base for k in range(3)]
    full = split3(jnp.concatenate(parts, 0))
    return jnp.concatenate([s[:8] for s in full], 0), jnp.concatenate(full, 0)


def gains(x, w, a, s):
    a = a[0:8] + (a[8:16] + a[16:24])
    s = s[0:32] + (s[32:64] + s[64:96])
    along = x[0:1] * w[0:1] + x[1:2] * w[1:2] + x[2:3] * w[2:3]
    t = along * s[0:8] - (w[0:1] * s[8:16] + w[1:2] * s[16:24] + w[2:3] * s[24:32])
    vel = (cross_rows(x, a[0:3]) - a[3:6]) * -inv_four_pi
    turn = cross_rows(x, t[0:3]) - t[3:6]
    stretch = (3.0 * inv_four_pi) * turn - inv_four_pi * cross_rows(w, a[0:3])
    return vel, stretch


def tile_rates(first, second, piece):
    n = first.shape[1]
    total = jnp.sum(first[0:3], axis=1, keepdims=True) + jnp.sum(second[0:3], axis=1, keepdims=True)
    centre = total * (0.5 / n)
    xp, xq = first[0:3] - centre, second[0:3] - centre
    wp, wq = first[3:6], second[3:6]
    sp, sq = 0.5 * first[6:7] * first[6:7], 0.5 * second[6:7] * second[6:7]
    bp, mp = moments(xp, wp)
    bq, mq = moments(xq, wq)
    cols = jnp.transpose(jnp.concatenate([first[0:3], sp, first[4:8]], 0))
    aq = jnp.zeros((24, n), f32)
    hq = jnp.zeros((96, n), f32)
    ap, hp = [], []
    dot = functools.partial(lax.dot_general, preferred_element_type=f32)
    for s in range(0, n, piece):
        cs = cols[s : s + piece]
        r = [cs[:, k : k + 1] - second[k : k + 1] for k in range(3)]
        g = r[0] * r[0] + r[1] * r[1] + r[2] * r[2] + (cs[:, 3:4] + sq)
        q = lax.rsqrt(g)
        q2 = q * q
        f = q2 * q
        h = f * q2
        fh, fl = split2(f)
        hh, hl = split2(h)
        f2, h2 = jnp.concatenate([fh, fl], 0), jnp.concatenate([hh, hl], 0)
        both = dot(f2, bq, NT)
        ap.append(both[:piece] + both[piece:])
        both = dot(h2, mq, NT)
        hp.append(both[:piece] + both[piece:])
        bps, mps = bp[:, s : s + piece], mp[:, s : s + piece]
        aq = aq + dot(jnp.concatenate([bps, bps], 1), f2, NN)
        hq = hq + dot(jnp.concatenate([mps, mps], 1), h2, NN)
    ap, hp = jnp.transpose(jnp.concatenate(ap, 0)), jnp.transpose(jnp.concatenate(hp, 0))
    return gains(xp, wp, ap, hp) + gains(xq, wq, aq, hq)


def place():
    gx, y = lax.axis_index("gx"), lax.axis_index("gy")
    return gx // N_J, lax.rem(gx, N_J), y


def wrap(v, n):
    return lax.rem(v + n, n)


J_STEPS = [(2, 0), (2, 1), (1, 0), (3, 0), (1, 1), (3, 1), (0, 1)]
Z_STEPS = [4, 3, 5, 2, 6, 1, 7]


def remote(src, dst, send, recv, device):
    return pltpu.make_async_remote_copy(
        src_ref=src, dst_ref=dst, send_sem=send, recv_sem=recv, device_id=device, device_id_type=MESH
    )


def number_of(storage):
    z, j = lax.shift_right_logical(storage, 5), lax.shift_right_logical(storage, 2) & (N_J - 1)
    return j * ROW + z * BLK_DEV + (storage & (BLK_DEV - 1))


def iota(shape, axis):
    return lax.broadcasted_iota(jnp.int32, shape, axis)


def dot32(a, b):
    return lax.dot_general(a, b, NN, preferred_element_type=f32)


def kernel(
    pairs_ref, home_ref, pairs_hbm, home_hbm, pos_hbm, str_hbm, rad_hbm, vel_out, str_out,
    table, pairs_vec, home_vec, pos_ref, str_ref, rad_ref, mix, own, grid, pack, named, part, team, final_team, dense, jin, fin, pick, final_pick,
    loads, os, orr, gs, gr, ts, tr, ps, pr, js, jr, fs, fr,
):
    z, j, y = place()
    x, core = j // 2, lax.rem(j, 2)
    gx = z * N_J + j
    me = z * N_Y + y
    other = (gx, wrap(y + 1, N_Y))
    active = y < 3

    def mate(i):
        tz, ty = wrap(z + i // N_Y, N_Z), wrap(y + i % N_Y, N_Y)
        return tz, ty, tz * N_Y + ty, (tz * N_J + j, ty)

    def mate_from(i):
        tz, ty = wrap(z - i // N_Y, N_Z), wrap(y - i % N_Y, N_Y)
        return ty, tz * N_Y + ty

    def near(step, way=1):
        dx, dc = step
        return wrap(x + way * dx, N_X) * 2 + lax.rem(core + dc, 2)

    incoming = [(pos_hbm, pos_ref), (str_hbm, str_ref), (rad_hbm, rad_ref)]
    incoming += [(pairs_hbm, pairs_vec), (home_hbm, home_vec)]
    incoming = [pltpu.make_async_copy(a, b, loads.at[i]) for i, (a, b) in enumerate(incoming)]
    for copy in incoming:
        copy.start()
    barrier = pltpu.get_barrier_semaphore()
    greeted = [(wrap(z + dz, N_Z) * N_J + j, y) for dz in Z_STEPS]
    greeted += [(gx, wrap(y + dy, N_Y)) for dy in (2, 1, 3)]
    greeted += [(z * N_J + near(step), y) for step in J_STEPS]
    for to in greeted:
        pl.semaphore_signal(barrier, inc=1, device_id=to, device_id_type=MESH)


    def enter(b, _):
        table[b] = number_of(home_ref[b])
        return 0

    lax.fori_loop(0, NB, enter, 0, unroll=8)
    for copy in incoming:
        copy.wait()
    rows_of = [(pos_ref, 0), (pos_ref, 1), (pos_ref, 2), (str_ref, 0), (str_ref, 1), (str_ref, 2)]
    for k, (ref, row) in enumerate(rows_of + [(rad_ref, 0)]):
        mix[k // 2, k % 2 : k % 2 + 1, :] = ref[row : row + 1, :]
    mix[3, 1:2, :] = jnp.zeros((1, BLK_DEV * BS), f32)
    for tz in range(N_Z):
        for b in range(BLK_DEV):
            own[tz, b] = mix[y, :, b * BS + tz * LANES : b * BS + (tz + 1) * LANES]

    pl.semaphore_wait(barrier, len(greeted))

    def home_of(tj, tz):
        return grid.at[pl.ds(tj * ROW + tz * BLK_DEV, BLK_DEV)]

    def row_of(tj):
        return grid.at[pl.ds(tj * ROW, ROW)]

    sends = []
    for i, dz in enumerate(Z_STEPS):
        tz = wrap(z + dz, N_Z)
        copy = remote(own.at[tz], home_of(j, z), os.at[i], orr.at[i], (tz * N_J + j, y))
        copy.start()
        sends.append(copy)
    for b in range(BLK_DEV):
        grid[j * ROW + z * BLK_DEV + b] = own[z, b]
    for i, dz in enumerate(Z_STEPS):
        there = home_of(j, wrap(z - dz, N_Z))
        remote(own.at[0], there, os.at[i], orr.at[i], other).wait_recv()
    for i, step in enumerate(J_STEPS):
        copy = remote(row_of(j), row_of(j), gs.at[i], gr.at[i], (z * N_J + near(step), y))
        copy.start()
        sends.append(copy)
    def numbers(lanes, row_at):
        chosen = jnp.where(iota((2 * TEAM * TILES_DEV * 4, lanes), 0) == row_at, 1.0, 0.0)
        logical = dot32(pairs_vec[...].astype(f32).astype(bf16), chosen.astype(bf16))
        home = jnp.broadcast_to(number_of(home_vec[...]), (8, NB)).astype(f32).astype(bf16)
        stored = []
        for k in range(2):
            match = jnp.where(iota((NB, lanes), 0).astype(f32) == logical[k : k + 1], 1.0, 0.0)
            stored.append(dot32(home, match.astype(bf16))[0:1])
        return stored

    r = iota((8 * N_J * N_Z, 1), 0)
    row_key = (((r // 8) * BLK_DEV + r % 4) * 2 + (r % 8) // 4).astype(f32)

    def one_hot(key):
        return jnp.where(row_key == key, 1.0, 0.0).astype(bf16)

    lanes = TEAM * TILES_DEV
    k = iota((1, lanes), 1)
    stored = numbers(lanes, ((k // 32) * N_J + j) * 32 + k % 32)
    for kc in range(4):
        pick[:, lanes * kc : lanes * (kc + 1)] = one_hot(stored[kc // 2] * 2.0 + kc % 2)
    late = TEAM * LATE
    k = iota((1, 4 * late), 1)
    m, t = (k % late) // LATE, EARLY + k % LATE
    stored = numbers(4 * late, ((m // N_Y) * N_J + j) * 32 + (m % N_Y) * TILES_DEV + t)
    key = jnp.where(k < 2 * late, stored[0], stored[1]) * 2.0 + ((k // late) % 2).astype(f32)
    final_pick[...] = one_hot(key)
    for m in range(TEAM):
        team[m, EARLY:] = jnp.zeros((LATE, 4, LANES), f32)
    for i, step in enumerate(J_STEPS):
        row = row_of(near(step, -1))
        remote(row, row, gs.at[i], gr.at[i], other).wait_recv()

    parts = ((0, 2), (2, 2), (4, TILES_DEV - 4))

    def block_of(tz, ty, t, k):
        row = (tz * N_J + j) * 32 + ty * TILES_DEV + t
        return table[pairs_ref[k, row]]

    def ask(i, g):
        at = pl.ds(*parts[g])
        return remote(pack.at[i, at], named.at[me, at], ts.at[g, i], tr.at[g, i], mate(i)[3])

    def asked(i, g):
        at = pl.ds(*parts[g])
        member = mate_from(i)[1]
        return remote(pack.at[i, at], named.at[member, at], ts.at[g, i], tr.at[g, i], other)

    for g, (t0, count) in enumerate(parts):

        def send(i, _, g=g, t0=t0, count=count):
            tz, ty, _, _ = mate(i)
            for t in range(t0, t0 + count):
                for k in range(2):
                    pack[i, t, 2 * k : 2 * k + 2, :] = grid[block_of(tz, ty, t, k)]
            ask(i, g).start()
            return 0

        if g == 0:
            for i in range(1, TEAM):
                send(i, 0)
        else:
            lax.fori_loop(1, TEAM, send, 0)
    for t in range(TILES_DEV):
        for k in range(2):
            named[me, t, 2 * k : 2 * k + 2, :] = grid[block_of(z, y, t, k)]

    lots = ((0, 4), (4, EARLY - 4), (EARLY, LATE))

    def give(i, g):
        at = pl.ds(*lots[g])
        _, _, member, to = mate(i)
        there = team.at[me, at] if g < 2 else final_team.at[me]
        return remote(part.at[member, at], there, ps.at[g, i], pr.at[g, i], to)

    def given(i, g):
        at = pl.ds(*lots[g])
        member = mate_from(i)[1]
        here = team.at[member, at] if g < 2 else final_team.at[member]
        return remote(part.at[0, at], here, ps.at[g, i], pr.at[g, i], other)

    def give_all(g):
        def send(i, _):
            @pl.when(mate(i)[1] < 3)
            def _():
                give(i, g).start()

            return 0

        if g == 2:
            for dy in range(N_Y):

                @pl.when(wrap(y + dy, N_Y) < 3)
                def _(dy=dy):
                    for i in range(dy if dy else N_Y, TEAM, N_Y):
                        give(i, g).start()
        else:
            lax.fori_loop(1, TEAM, send, 0)

    def wait_asked(g):
        def wait(i, _):
            asked(i, g).wait_recv()
            return 0

        lax.fori_loop(1, TEAM, wait, 0)

    def two_tiles(pair, _):
        t = 2 * pair
        for g, (t0, _count) in enumerate(parts):
            pl.when(t == t0)(functools.partial(wait_asked, g))

        def rows(t, k):
            pieces = []
            for e in range(N_Z):
                pairs_of = [named[e * N_Y + q, t, 2 * k : 2 * k + 2, :] for q in range(N_Y)]
                pieces.append(jnp.concatenate(pairs_of, 0))
            return jnp.concatenate(pieces, 1)

        rates = [tile_rates(rows(t + u, 0), rows(t + u, 1), 128) for u in range(2)]
        for u in range(2):
            v1, s1, v2, s2 = rates[u]
            for k, v, st in ((0, v1, s1), (1, v2, s2)):
                full = jnp.concatenate([v, st], 0)
                for q in range(3):
                    for e in range(N_Z):
                        piece = full[2 * q : 2 * q + 2, LANES * e : LANES * (e + 1)]
                        part[e * N_Y + q, t + u, 2 * k : 2 * k + 2, :] = piece
        for g, (t0, count) in enumerate(lots):
            pl.when(t + 2 == t0 + count)(functools.partial(give_all, g))
        return 0

    lax.fori_loop(0, TILES_DEV // 2, two_tiles, 0)

    def by_block(chosen, terms):
        sums = dot32(chosen, jnp.concatenate(split3(terms), 1))
        return sums[:, 0:LANES] + (sums[:, LANES : 2 * LANES] + sums[:, 2 * LANES :])

    @pl.when(active)
    def _():
        team[me, 0:EARLY] = part[me, 0:EARLY]
        final_team[me] = part[me, EARLY:]

        def wait(g, i, _):
            given(i, g).wait_recv()
            return 0

        lax.fori_loop(1, TEAM, functools.partial(wait, 0), 0)
        lax.fori_loop(1, TEAM, functools.partial(wait, 1), 0)
        lanes = TEAM * TILES_DEV
        terms = jnp.concatenate([team[:, :, kc, :].reshape(lanes, LANES) for kc in range(4)], 0)
        sums = by_block(pick[...], terms)
        lax.fori_loop(1, TEAM, functools.partial(wait, 2), 0)
        terms = [final_team[:, :, kc, :].reshape(TEAM * LATE, LANES) for kc in range(4)]
        terms = jnp.concatenate(terms, 0)
        sums = sums + by_block(final_pick[...], terms)
        dense[...] = sums.reshape(N_J, N_Z, 8, LANES)
        for i, step in enumerate(J_STEPS):
            tj = near(step)
            remote(dense.at[tj], jin.at[i], js.at[i], jr.at[i], (z * N_J + tj, y)).start()
        for i in range(7):
            remote(dense.at[0], jin.at[i], js.at[i], jr.at[i], other).wait_recv()
        total = dense[j]
        for i in range(7):
            total = total + jin[i]
        dense[j] = total
        fin[me] = dense[j, z]

        for i in range(1, TEAM):
            tz, _, _, to = mate(i)
            remote(dense.at[j, tz], fin.at[me], fs.at[i], fr.at[i], to).start()

    def settle(i, _):
        for g in range(3):
            ask(i, g).wait_send()

        @pl.when(mate(i)[1] < 3)
        def _():
            for g in range(3):
                give(i, g).wait_send()

        return 0

    lax.fori_loop(1, TEAM, settle, 0)
    for copy in sends:
        copy.wait_send()

    @pl.when(active)
    def _():
        for i, step in enumerate(J_STEPS):
            remote(dense.at[near(step)], jin.at[i], js.at[i], jr.at[i], other).wait_send()

    def last(i, _):
        from_y, member = mate_from(i)

        @pl.when(from_y < 3)
        def _():
            remote(dense.at[0, 0], fin.at[member], fs.at[i], fr.at[i], other).wait_recv()

        @pl.when(active)
        def _():
            tz, _, _, to = mate(i)
            remote(dense.at[j, tz], fin.at[me], fs.at[i], fr.at[i], to).wait_send()

        return 0

    lax.fori_loop(1, TEAM, last, 0)
    outs = [(vel_out, 0), (vel_out, 1), (vel_out, 2), (str_out, 0), (str_out, 1), (str_out, 2)]
    for q in range(3):
        for e in range(N_Z):
            full = fin[e * N_Y + q]
            for c in range(2):
                ref, row = outs[2 * q + c]
                for b in range(BLK_DEV):
                    at = slice(b * BS + e * LANES, b * BS + (e + 1) * LANES)
                    ref[row : row + 1, at] = full[c * 4 + b : c * 4 + b + 1]


def run(pairs, home, positions, strengths, radii):
    vmem, smem = pl.BlockSpec(memory_space=pltpu.VMEM), pl.BlockSpec(memory_space=pltpu.SMEM)
    dma = pltpu.SemaphoreType.DMA
    out = jax.ShapeDtypeStruct((3, BLK_DEV * BS), f32)
    n = BLK_DEV * BS
    words = [(2, 2 * TEAM * TILES_DEV * 4), (1, NB)]
    buffers = [
        (3, n),
        (3, n),
        (1, n),
        (N_Y, 2, BLK_DEV * BS),
        (N_Z, BLK_DEV, 2, LANES),
        (NB, 2, LANES),
        (TEAM, TILES_DEV, 4, LANES),
        (TEAM, TILES_DEV, 4, LANES),
        (TEAM, TILES_DEV, 4, LANES),
        (TEAM, TILES_DEV, 4, LANES),
        (TEAM, LATE, 4, LANES),
        (N_J, N_Z, 8, LANES),
        (7, N_Z, 8, LANES),
        (TEAM, 8, LANES),
    ]
    chosen = [(8 * N_J * N_Z, 4 * TEAM * TILES_DEV), (8 * N_J * N_Z, 4 * TEAM * LATE)]
    counts = [(7,), (7,), (3, TEAM), (3, TEAM), (7,), (TEAM,)]
    return pl.pallas_call(
        kernel,
        out_shape=(out, out),
        in_specs=[smem, smem] + [pl.BlockSpec(memory_space=pl.ANY)] * 5,
        out_specs=(vmem, vmem),
        scratch_shapes=[pltpu.SMEM((NB,), jnp.int32)]
        + [pltpu.VMEM(b, jnp.int32) for b in words]
        + [pltpu.VMEM(b, f32) for b in buffers]
        + [pltpu.VMEM(b, bf16) for b in chosen]
        + [dma((5,))]
        + [dma(c) for c in counts for _ in range(2)],
        compiler_params=pltpu.CompilerParams(
            collective_id=0, has_side_effects=True, vmem_limit_bytes=63 * 2**20
        ),
    )(pairs, home, pairs, home[None, :], positions, strengths, radii)


def body(positions, strengths, core_radii, tile_pairs, block_home):
    return run(tile_pairs.T, block_home, positions, strengths, core_radii[None, :])


def solution(mesh):
    return jax.shard_map(
        body,
        mesh=mesh,
        in_specs=(P(None, "gx"), P(None, "gx"), P("gx"), P(), P()),
        out_specs=(P(None, "gx"), P(None, "gx")),
        check_vma=False,
    )
```

```python
import functools

import jax
import jax.numpy as jnp
from jax import lax
from jax.experimental import pallas as pl
from jax.experimental.pallas import tpu as pltpu
from jax.sharding import PartitionSpec as P

BS = 1024
TILES_DEV = 8
BLK_DEV = 4
N_Z, N_X, N_CORE, N_Y = 8, 4, 2, 4
N_J = N_X * N_CORE
TEAM = N_Z * N_Y
SLOTS = 2 * TILES_DEV
NB = 256
ROW = BLK_DEV * N_Z
EARLY = TILES_DEV - 2
LATE = TILES_DEV - EARLY
LANES = 128
MESH = pl.DeviceIdType.MESH

inv_four_pi = 0.07957747154594767
f32, bf16 = jnp.float32, jnp.bfloat16
NT = (((1,), (1,)), ((), ()))
NN = (((1,), (0,)), ((), ()))


def split3(a):
    hi = a.astype(bf16)
    rest = a - hi.astype(f32)
    mid = rest.astype(bf16)
    lo = (rest - mid.astype(f32)).astype(bf16)
    return hi, mid, lo


def split2(v):
    hi = v.astype(bf16)
    return hi, (v - hi.astype(f32)).astype(bf16)


def cross_rows(a, b):
    a0, a1, a2 = (a[k : k + 1] for k in range(3))
    b0, b1, b2 = (b[k : k + 1] for k in range(3))
    return jnp.concatenate([a1 * b2 - a2 * b1, a2 * b0 - a0 * b2, a0 * b1 - a1 * b0], 0)


def moments(x, w):
    base = jnp.concatenate([w, cross_rows(x, w), jnp.zeros((2, w.shape[1]), f32)], 0)
    parts = [base] + [x[k : k + 1] * base for k in range(3)]
    full = split3(jnp.concatenate(parts, 0))
    return jnp.concatenate([s[:8] for s in full], 0), jnp.concatenate(full, 0)


def gains(x, w, a, s):
    a = a[0:8] + (a[8:16] + a[16:24])
    s = s[0:32] + (s[32:64] + s[64:96])
    along = x[0:1] * w[0:1] + x[1:2] * w[1:2] + x[2:3] * w[2:3]
    t = along * s[0:8] - (w[0:1] * s[8:16] + w[1:2] * s[16:24] + w[2:3] * s[24:32])
    vel = (cross_rows(x, a[0:3]) - a[3:6]) * -inv_four_pi
    turn = cross_rows(x, t[0:3]) - t[3:6]
    stretch = (3.0 * inv_four_pi) * turn - inv_four_pi * cross_rows(w, a[0:3])
    return vel, stretch


def tile_rates(first, second, piece):
    n = first.shape[1]
    total = jnp.sum(first[0:3], axis=1, keepdims=True) + jnp.sum(second[0:3], axis=1, keepdims=True)
    centre = total * (0.5 / n)
    xp, xq = first[0:3] - centre, second[0:3] - centre
    wp, wq = first[3:6], second[3:6]
    sp, sq = 0.5 * first[6:7] * first[6:7], 0.5 * second[6:7] * second[6:7]
    bp, mp = moments(xp, wp)
    bq, mq = moments(xq, wq)
    cols = jnp.transpose(jnp.concatenate([first[0:3], sp, first[4:8]], 0))
    aq = jnp.zeros((24, n), f32)
    hq = jnp.zeros((96, n), f32)
    ap, hp = [], []
    dot = functools.partial(lax.dot_general, preferred_element_type=f32)
    for s in range(0, n, piece):
        cs = cols[s : s + piece]
        r = [cs[:, k : k + 1] - second[k : k + 1] for k in range(3)]
        g = r[0] * r[0] + r[1] * r[1] + r[2] * r[2] + (cs[:, 3:4] + sq)
        q = lax.rsqrt(g)
        q2 = q * q
        f = q2 * q
        h = f * q2
        fh, fl = split2(f)
        hh, hl = split2(h)
        f2, h2 = jnp.concatenate([fh, fl], 0), jnp.concatenate([hh, hl], 0)
        both = dot(f2, bq, NT)
        ap.append(both[:piece] + both[piece:])
        both = dot(h2, mq, NT)
        hp.append(both[:piece] + both[piece:])
        bps, mps = bp[:, s : s + piece], mp[:, s : s + piece]
        aq = aq + dot(jnp.concatenate([bps, bps], 1), f2, NN)
        hq = hq + dot(jnp.concatenate([mps, mps], 1), h2, NN)
    ap, hp = jnp.transpose(jnp.concatenate(ap, 0)), jnp.transpose(jnp.concatenate(hp, 0))
    return gains(xp, wp, ap, hp) + gains(xq, wq, aq, hq)


def place():
    gx, y = lax.axis_index("gx"), lax.axis_index("gy")
    return gx // N_J, lax.rem(gx, N_J), y


def wrap(v, n):
    return lax.rem(v + n, n)


J_STEPS = [(2, 0), (2, 1), (1, 0), (3, 0), (1, 1), (3, 1), (0, 1)]
Z_STEPS = [4, 3, 5, 2, 6, 1, 7]


def remote(src, dst, send, recv, device):
    return pltpu.make_async_remote_copy(
        src_ref=src, dst_ref=dst, send_sem=send, recv_sem=recv, device_id=device, device_id_type=MESH
    )


def number_of(storage):
    z, j = lax.shift_right_logical(storage, 5), lax.shift_right_logical(storage, 2) & (N_J - 1)
    return j * ROW + z * BLK_DEV + (storage & (BLK_DEV - 1))


def iota(shape, axis):
    return lax.broadcasted_iota(jnp.int32, shape, axis)


def dot32(a, b):
    return lax.dot_general(a, b, NN, preferred_element_type=f32)


def kernel(
    pairs_ref, home_ref, pairs_hbm, home_hbm, pos_hbm, str_hbm, rad_hbm, vel_out, str_out,
    table, pairs_vec, home_vec, pos_ref, str_ref, rad_ref, mix, own, grid, pack, named, part, team, final_team, dense, jin, fin, pick, final_pick,
    loads, os, orr, gs, gr, ts, tr, ps, pr, js, jr, fs, fr,
):
    z, j, y = place()
    x, core = j // 2, lax.rem(j, 2)
    gx = z * N_J + j
    me = z * N_Y + y
    other = (gx, wrap(y + 1, N_Y))
    active = y < 3

    def mate(i):
        tz, ty = wrap(z + i // N_Y, N_Z), wrap(y + i % N_Y, N_Y)
        return tz, ty, tz * N_Y + ty, (tz * N_J + j, ty)

    def mate_from(i):
        tz, ty = wrap(z - i // N_Y, N_Z), wrap(y - i % N_Y, N_Y)
        return ty, tz * N_Y + ty

    def near(step, way=1):
        dx, dc = step
        return wrap(x + way * dx, N_X) * 2 + lax.rem(core + dc, 2)

    incoming = [(pos_hbm, pos_ref), (str_hbm, str_ref), (rad_hbm, rad_ref)]
    incoming += [(pairs_hbm, pairs_vec), (home_hbm, home_vec)]
    incoming = [pltpu.make_async_copy(a, b, loads.at[i]) for i, (a, b) in enumerate(incoming)]
    for copy in incoming:
        copy.start()
    barrier = pltpu.get_barrier_semaphore()
    greeted = [(wrap(z + dz, N_Z) * N_J + j, y) for dz in Z_STEPS]
    greeted += [(gx, wrap(y + dy, N_Y)) for dy in (2, 1, 3)]
    greeted += [(z * N_J + near(step), y) for step in J_STEPS]
    for to in greeted:
        pl.semaphore_signal(barrier, inc=1, device_id=to, device_id_type=MESH)


    for copy in incoming:
        copy.wait()
    rows_of = [(pos_ref, 0), (pos_ref, 1), (pos_ref, 2), (str_ref, 0), (str_ref, 1), (str_ref, 2)]
    for k, (ref, row) in enumerate(rows_of + [(rad_ref, 0)]):
        mix[k // 2, k % 2 : k % 2 + 1, :] = ref[row : row + 1, :]
    mix[3, 1:2, :] = jnp.zeros((1, BLK_DEV * BS), f32)
    for tz in range(N_Z):
        for b in range(BLK_DEV):
            own[tz, b] = mix[y, :, b * BS + tz * LANES : b * BS + (tz + 1) * LANES]

    pl.semaphore_wait(barrier, len(greeted))

    def home_of(tj, tz):
        return grid.at[pl.ds(tj * ROW + tz * BLK_DEV, BLK_DEV)]

    def row_of(tj):
        return grid.at[pl.ds(tj * ROW, ROW)]

    sends = []
    for i, dz in enumerate(Z_STEPS):
        tz = wrap(z + dz, N_Z)
        copy = remote(own.at[tz], home_of(j, z), os.at[i], orr.at[i], (tz * N_J + j, y))
        copy.start()
        sends.append(copy)
    for b in range(BLK_DEV):
        grid[j * ROW + z * BLK_DEV + b] = own[z, b]
    for i, dz in enumerate(Z_STEPS):
        there = home_of(j, wrap(z - dz, N_Z))
        remote(own.at[0], there, os.at[i], orr.at[i], other).wait_recv()
    for i, step in enumerate(J_STEPS):
        copy = remote(row_of(j), row_of(j), gs.at[i], gr.at[i], (z * N_J + near(step), y))
        copy.start()
        sends.append(copy)
    def enter(b, _):
        table[b] = number_of(home_ref[b])
        return 0

    lax.fori_loop(0, NB, enter, 0, unroll=8)

    def numbers(lanes, row_at):
        chosen = jnp.where(iota((2 * TEAM * TILES_DEV * 4, lanes), 0) == row_at, 1.0, 0.0)
        logical = dot32(pairs_vec[...].astype(f32).astype(bf16), chosen.astype(bf16))
        home = jnp.broadcast_to(number_of(home_vec[...]), (8, NB)).astype(f32).astype(bf16)
        stored = []
        for k in range(2):
            match = jnp.where(iota((NB, lanes), 0).astype(f32) == logical[k : k + 1], 1.0, 0.0)
            stored.append(dot32(home, match.astype(bf16))[0:1])
        return stored

    r = iota((8 * N_J * N_Z, 1), 0)
    row_key = (((r // 8) * BLK_DEV + r % 4) * 2 + (r % 8) // 4).astype(f32)

    def one_hot(key):
        return jnp.where(row_key == key, 1.0, 0.0).astype(bf16)

    lanes = TEAM * TILES_DEV
    k = iota((1, lanes), 1)
    stored = numbers(lanes, ((k // 32) * N_J + j) * 32 + k % 32)
    for kc in range(4):
        pick[:, lanes * kc : lanes * (kc + 1)] = one_hot(stored[kc // 2] * 2.0 + kc % 2)
    late = TEAM * LATE
    k = iota((1, 4 * late), 1)
    m, t = (k % late) // LATE, EARLY + k % LATE
    stored = numbers(4 * late, ((m // N_Y) * N_J + j) * 32 + (m % N_Y) * TILES_DEV + t)
    key = jnp.where(k < 2 * late, stored[0], stored[1]) * 2.0 + ((k // late) % 2).astype(f32)
    final_pick[...] = one_hot(key)
    for m in range(TEAM):
        team[m, EARLY:] = jnp.zeros((LATE, 4, LANES), f32)
    for i, step in enumerate(J_STEPS):
        row = row_of(near(step, -1))
        remote(row, row, gs.at[i], gr.at[i], other).wait_recv()

    parts = ((0, 2), (2, 2), (4, TILES_DEV - 4))

    def block_of(tz, ty, t, k):
        row = (tz * N_J + j) * 32 + ty * TILES_DEV + t
        return table[pairs_ref[k, row]]

    def ask(i, g):
        at = pl.ds(*parts[g])
        return remote(pack.at[i, at], named.at[me, at], ts.at[g, i], tr.at[g, i], mate(i)[3])

    def asked(i, g):
        at = pl.ds(*parts[g])
        member = mate_from(i)[1]
        return remote(pack.at[i, at], named.at[member, at], ts.at[g, i], tr.at[g, i], other)

    for g, (t0, count) in enumerate(parts):

        def send(i, g=g, t0=t0, count=count):
            tz, ty, _, _ = mate(i)
            for t in range(t0, t0 + count):
                for k in range(2):
                    pack[i, t, 2 * k : 2 * k + 2, :] = grid[block_of(tz, ty, t, k)]
            ask(i, g).start()

        for i in range(1, TEAM):
            send(i)
    for t in range(TILES_DEV):
        for k in range(2):
            named[me, t, 2 * k : 2 * k + 2, :] = grid[block_of(z, y, t, k)]

    lots = ((0, 4), (4, EARLY - 4), (EARLY, LATE))

    def give(i, g):
        at = pl.ds(*lots[g])
        _, _, member, to = mate(i)
        there = team.at[me, at] if g < 2 else final_team.at[me]
        return remote(part.at[member, at], there, ps.at[g, i], pr.at[g, i], to)

    def given(i, g):
        at = pl.ds(*lots[g])
        member = mate_from(i)[1]
        here = team.at[member, at] if g < 2 else final_team.at[member]
        return remote(part.at[0, at], here, ps.at[g, i], pr.at[g, i], other)

    def give_all(g):
        for dy in range(N_Y):

            @pl.when(wrap(y + dy, N_Y) < 3)
            def _(dy=dy):
                for i in range(dy if dy else N_Y, TEAM, N_Y):
                    give(i, g).start()

    def wait_asked(g):
        def wait(i, _):
            asked(i, g).wait_recv()
            return 0

        lax.fori_loop(1, TEAM, wait, 0)

    def two_tiles(pair, _):
        t = 2 * pair
        for g, (t0, _count) in enumerate(parts):
            pl.when(t == t0)(functools.partial(wait_asked, g))

        def rows(t, k):
            pieces = []
            for e in range(N_Z):
                pairs_of = [named[e * N_Y + q, t, 2 * k : 2 * k + 2, :] for q in range(N_Y)]
                pieces.append(jnp.concatenate(pairs_of, 0))
            return jnp.concatenate(pieces, 1)

        rates = [tile_rates(rows(t + u, 0), rows(t + u, 1), 128) for u in range(2)]
        for u in range(2):
            v1, s1, v2, s2 = rates[u]
            for k, v, st in ((0, v1, s1), (1, v2, s2)):
                full = jnp.concatenate([v, st], 0)
                for q in range(3):
                    for e in range(N_Z):
                        piece = full[2 * q : 2 * q + 2, LANES * e : LANES * (e + 1)]
                        part[e * N_Y + q, t + u, 2 * k : 2 * k + 2, :] = piece
        for g, (t0, count) in enumerate(lots):
            pl.when(t + 2 == t0 + count)(functools.partial(give_all, g))
        return 0

    lax.fori_loop(0, TILES_DEV // 2, two_tiles, 0)

    def by_block(chosen, terms):
        sums = dot32(chosen, jnp.concatenate(split3(terms), 1))
        return sums[:, 0:LANES] + (sums[:, LANES : 2 * LANES] + sums[:, 2 * LANES :])

    @pl.when(active)
    def _():
        team[me, 0:EARLY] = part[me, 0:EARLY]
        final_team[me] = part[me, EARLY:]

        def wait(g, i, _):
            given(i, g).wait_recv()
            return 0

        lax.fori_loop(1, TEAM, functools.partial(wait, 0), 0)
        lax.fori_loop(1, TEAM, functools.partial(wait, 1), 0)
        lanes = TEAM * TILES_DEV
        terms = jnp.concatenate([team[:, :, kc, :].reshape(lanes, LANES) for kc in range(4)], 0)
        sums = by_block(pick[...], terms)
        lax.fori_loop(1, TEAM, functools.partial(wait, 2), 0)
        terms = [final_team[:, :, kc, :].reshape(TEAM * LATE, LANES) for kc in range(4)]
        terms = jnp.concatenate(terms, 0)
        sums = sums + by_block(final_pick[...], terms)
        dense[...] = sums.reshape(N_J, N_Z, 8, LANES)
        for i, step in enumerate(J_STEPS):
            tj = near(step)
            remote(dense.at[tj], jin.at[i], js.at[i], jr.at[i], (z * N_J + tj, y)).start()
        for i in range(7):
            remote(dense.at[0], jin.at[i], js.at[i], jr.at[i], other).wait_recv()
        total = dense[j]
        for i in range(7):
            total = total + jin[i]
        dense[j] = total
        fin[me] = dense[j, z]

        for i in range(1, TEAM):
            tz, _, _, to = mate(i)
            remote(dense.at[j, tz], fin.at[me], fs.at[i], fr.at[i], to).start()

    def settle(i, _):
        for g in range(3):
            ask(i, g).wait_send()

        @pl.when(mate(i)[1] < 3)
        def _():
            for g in range(3):
                give(i, g).wait_send()

        return 0

    lax.fori_loop(1, TEAM, settle, 0)
    for copy in sends:
        copy.wait_send()

    @pl.when(active)
    def _():
        for i, step in enumerate(J_STEPS):
            remote(dense.at[near(step)], jin.at[i], js.at[i], jr.at[i], other).wait_send()

    def last(i, _):
        from_y, member = mate_from(i)

        @pl.when(from_y < 3)
        def _():
            remote(dense.at[0, 0], fin.at[member], fs.at[i], fr.at[i], other).wait_recv()

        @pl.when(active)
        def _():
            tz, _, _, to = mate(i)
            remote(dense.at[j, tz], fin.at[me], fs.at[i], fr.at[i], to).wait_send()

        return 0

    lax.fori_loop(1, TEAM, last, 0)
    outs = [(vel_out, 0), (vel_out, 1), (vel_out, 2), (str_out, 0), (str_out, 1), (str_out, 2)]
    for q in range(3):
        for e in range(N_Z):
            full = fin[e * N_Y + q]
            for c in range(2):
                ref, row = outs[2 * q + c]
                for b in range(BLK_DEV):
                    at = slice(b * BS + e * LANES, b * BS + (e + 1) * LANES)
                    ref[row : row + 1, at] = full[c * 4 + b : c * 4 + b + 1]


def run(pairs, home, positions, strengths, radii):
    vmem, smem = pl.BlockSpec(memory_space=pltpu.VMEM), pl.BlockSpec(memory_space=pltpu.SMEM)
    dma = pltpu.SemaphoreType.DMA
    out = jax.ShapeDtypeStruct((3, BLK_DEV * BS), f32)
    n = BLK_DEV * BS
    words = [(2, 2 * TEAM * TILES_DEV * 4), (1, NB)]
    buffers = [
        (3, n),
        (3, n),
        (1, n),
        (N_Y, 2, BLK_DEV * BS),
        (N_Z, BLK_DEV, 2, LANES),
        (NB, 2, LANES),
        (TEAM, TILES_DEV, 4, LANES),
        (TEAM, TILES_DEV, 4, LANES),
        (TEAM, TILES_DEV, 4, LANES),
        (TEAM, TILES_DEV, 4, LANES),
        (TEAM, LATE, 4, LANES),
        (N_J, N_Z, 8, LANES),
        (7, N_Z, 8, LANES),
        (TEAM, 8, LANES),
    ]
    chosen = [(8 * N_J * N_Z, 4 * TEAM * TILES_DEV), (8 * N_J * N_Z, 4 * TEAM * LATE)]
    counts = [(7,), (7,), (3, TEAM), (3, TEAM), (7,), (TEAM,)]
    return pl.pallas_call(
        kernel,
        out_shape=(out, out),
        in_specs=[smem, smem] + [pl.BlockSpec(memory_space=pl.ANY)] * 5,
        out_specs=(vmem, vmem),
        scratch_shapes=[pltpu.SMEM((NB,), jnp.int32)]
        + [pltpu.VMEM(b, jnp.int32) for b in words]
        + [pltpu.VMEM(b, f32) for b in buffers]
        + [pltpu.VMEM(b, bf16) for b in chosen]
        + [dma((5,))]
        + [dma(c) for c in counts for _ in range(2)],
        compiler_params=pltpu.CompilerParams(
            collective_id=0, has_side_effects=True, vmem_limit_bytes=63 * 2**20
        ),
    )(pairs, home, pairs, home[None, :], positions, strengths, radii)


def body(positions, strengths, core_radii, tile_pairs, block_home):
    return run(tile_pairs.T, block_home, positions, strengths, core_radii[None, :])


def solution(mesh):
    return jax.shard_map(
        body,
        mesh=mesh,
        in_specs=(P(None, "gx"), P(None, "gx"), P("gx"), P(), P()),
        out_specs=(P(None, "gx"), P(None, "gx")),
        check_vma=False,
    )
```

```python
import functools

import jax
import jax.numpy as jnp
from jax import lax
from jax.experimental import pallas as pl
from jax.experimental.pallas import tpu as pltpu
from jax.sharding import PartitionSpec as P

BS = 1024
TILES_DEV = 8
BLK_DEV = 4
N_Z, N_X, N_CORE, N_Y = 8, 4, 2, 4
N_J = N_X * N_CORE
TEAM = N_Z * N_Y
SLOTS = 2 * TILES_DEV
NB = 256
ROW = BLK_DEV * N_Z
EARLY = TILES_DEV - 2
LATE = TILES_DEV - EARLY
LANES = 128
MESH = pl.DeviceIdType.MESH

inv_four_pi = 0.07957747154594767
f32, bf16 = jnp.float32, jnp.bfloat16
NT = (((1,), (1,)), ((), ()))
NN = (((1,), (0,)), ((), ()))


def split3(a):
    hi = a.astype(bf16)
    rest = a - hi.astype(f32)
    mid = rest.astype(bf16)
    lo = (rest - mid.astype(f32)).astype(bf16)
    return hi, mid, lo


def split2(v):
    hi = v.astype(bf16)
    return hi, (v - hi.astype(f32)).astype(bf16)


def cross_rows(a, b):
    a0, a1, a2 = (a[k : k + 1] for k in range(3))
    b0, b1, b2 = (b[k : k + 1] for k in range(3))
    return jnp.concatenate([a1 * b2 - a2 * b1, a2 * b0 - a0 * b2, a0 * b1 - a1 * b0], 0)


def moments(x, w):
    base = jnp.concatenate([w, cross_rows(x, w), jnp.zeros((2, w.shape[1]), f32)], 0)
    parts = [base] + [x[k : k + 1] * base for k in range(3)]
    full = split3(jnp.concatenate(parts, 0))
    return jnp.concatenate([s[:8] for s in full], 0), jnp.concatenate(full, 0)


def gains(x, w, a, s):
    a = a[0:8] + (a[8:16] + a[16:24])
    s = s[0:32] + (s[32:64] + s[64:96])
    along = x[0:1] * w[0:1] + x[1:2] * w[1:2] + x[2:3] * w[2:3]
    t = along * s[0:8] - (w[0:1] * s[8:16] + w[1:2] * s[16:24] + w[2:3] * s[24:32])
    vel = (cross_rows(x, a[0:3]) - a[3:6]) * -inv_four_pi
    turn = cross_rows(x, t[0:3]) - t[3:6]
    stretch = (3.0 * inv_four_pi) * turn - inv_four_pi * cross_rows(w, a[0:3])
    return vel, stretch


def tile_rates(first, second, piece):
    n = first.shape[1]
    total = jnp.sum(first[0:3], axis=1, keepdims=True) + jnp.sum(second[0:3], axis=1, keepdims=True)
    centre = total * (0.5 / n)
    xp, xq = first[0:3] - centre, second[0:3] - centre
    wp, wq = first[3:6], second[3:6]
    sp, sq = 0.5 * first[6:7] * first[6:7], 0.5 * second[6:7] * second[6:7]
    bp, mp = moments(xp, wp)
    bq, mq = moments(xq, wq)
    cols = jnp.transpose(jnp.concatenate([first[0:3], sp, first[4:8]], 0))
    aq = jnp.zeros((24, n), f32)
    hq = jnp.zeros((96, n), f32)
    ap, hp = [], []
    dot = functools.partial(lax.dot_general, preferred_element_type=f32)
    for s in range(0, n, piece):
        cs = cols[s : s + piece]
        r = [cs[:, k : k + 1] - second[k : k + 1] for k in range(3)]
        g = r[0] * r[0] + r[1] * r[1] + r[2] * r[2] + (cs[:, 3:4] + sq)
        q = lax.rsqrt(g)
        q2 = q * q
        f = q2 * q
        h = f * q2
        fh, fl = split2(f)
        hh, hl = split2(h)
        f2, h2 = jnp.concatenate([fh, fl], 0), jnp.concatenate([hh, hl], 0)
        both = dot(f2, bq, NT)
        ap.append(both[:piece] + both[piece:])
        both = dot(h2, mq, NT)
        hp.append(both[:piece] + both[piece:])
        bps, mps = bp[:, s : s + piece], mp[:, s : s + piece]
        aq = aq + dot(jnp.concatenate([bps, bps], 1), f2, NN)
        hq = hq + dot(jnp.concatenate([mps, mps], 1), h2, NN)
    ap, hp = jnp.transpose(jnp.concatenate(ap, 0)), jnp.transpose(jnp.concatenate(hp, 0))
    return gains(xp, wp, ap, hp) + gains(xq, wq, aq, hq)


def place():
    gx, y = lax.axis_index("gx"), lax.axis_index("gy")
    return gx // N_J, lax.rem(gx, N_J), y


def wrap(v, n):
    return lax.rem(v + n, n)


J_STEPS = [(2, 0), (2, 1), (1, 0), (3, 0), (1, 1), (3, 1), (0, 1)]
Z_STEPS = [4, 3, 5, 2, 6, 1, 7]
MATES = [dz * N_Y + dy for dz in Z_STEPS + [0] for dy in (2, 1, 3, 0) if dz or dy]


def remote(src, dst, send, recv, device):
    return pltpu.make_async_remote_copy(
        src_ref=src, dst_ref=dst, send_sem=send, recv_sem=recv, device_id=device, device_id_type=MESH
    )


def number_of(storage):
    z, j = lax.shift_right_logical(storage, 5), lax.shift_right_logical(storage, 2) & (N_J - 1)
    return j * ROW + z * BLK_DEV + (storage & (BLK_DEV - 1))


def iota(shape, axis):
    return lax.broadcasted_iota(jnp.int32, shape, axis)


def dot32(a, b):
    return lax.dot_general(a, b, NN, preferred_element_type=f32)


def kernel(
    pairs_ref, home_ref, pairs_hbm, home_hbm, pos_hbm, str_hbm, rad_hbm, vel_out, str_out,
    table, pairs_vec, home_vec, pos_ref, str_ref, rad_ref, mix, own, grid, pack, named, part, team, final_team, dense, jin, fin, pick, final_pick,
    loads, os, orr, gs, gr, ts, tr, ps, pr, js, jr, fs, fr,
):
    z, j, y = place()
    x, core = j // 2, lax.rem(j, 2)
    gx = z * N_J + j
    me = z * N_Y + y
    other = (gx, wrap(y + 1, N_Y))
    active = y < 3

    def mate(i):
        tz, ty = wrap(z + i // N_Y, N_Z), wrap(y + i % N_Y, N_Y)
        return tz, ty, tz * N_Y + ty, (tz * N_J + j, ty)

    def mate_from(i):
        tz, ty = wrap(z - i // N_Y, N_Z), wrap(y - i % N_Y, N_Y)
        return ty, tz * N_Y + ty

    def near(step, way=1):
        dx, dc = step
        return wrap(x + way * dx, N_X) * 2 + lax.rem(core + dc, 2)

    incoming = [(pos_hbm, pos_ref), (str_hbm, str_ref), (rad_hbm, rad_ref)]
    incoming += [(pairs_hbm, pairs_vec), (home_hbm, home_vec)]
    incoming = [pltpu.make_async_copy(a, b, loads.at[i]) for i, (a, b) in enumerate(incoming)]
    for copy in incoming:
        copy.start()
    barrier = pltpu.get_barrier_semaphore()
    greeted = [(wrap(z + dz, N_Z) * N_J + j, y) for dz in Z_STEPS]
    greeted += [(gx, wrap(y + dy, N_Y)) for dy in (2, 1, 3)]
    greeted += [(z * N_J + near(step), y) for step in J_STEPS]
    for to in greeted:
        pl.semaphore_signal(barrier, inc=1, device_id=to, device_id_type=MESH)


    for copy in incoming:
        copy.wait()
    rows_of = [(pos_ref, 0), (pos_ref, 1), (pos_ref, 2), (str_ref, 0), (str_ref, 1), (str_ref, 2)]
    for k, (ref, row) in enumerate(rows_of + [(rad_ref, 0)]):
        mix[k // 2, k % 2 : k % 2 + 1, :] = ref[row : row + 1, :]
    mix[3, 1:2, :] = jnp.zeros((1, BLK_DEV * BS), f32)
    for tz in range(N_Z):
        for b in range(BLK_DEV):
            own[tz, b] = mix[y, :, b * BS + tz * LANES : b * BS + (tz + 1) * LANES]

    pl.semaphore_wait(barrier, len(greeted))

    def home_of(tj, tz):
        return grid.at[pl.ds(tj * ROW + tz * BLK_DEV, BLK_DEV)]

    def row_of(tj):
        return grid.at[pl.ds(tj * ROW, ROW)]

    sends = []
    for i, dz in enumerate(Z_STEPS):
        tz = wrap(z + dz, N_Z)
        copy = remote(own.at[tz], home_of(j, z), os.at[i], orr.at[i], (tz * N_J + j, y))
        copy.start()
        sends.append(copy)
    for b in range(BLK_DEV):
        grid[j * ROW + z * BLK_DEV + b] = own[z, b]
    for i, dz in enumerate(Z_STEPS):
        there = home_of(j, wrap(z - dz, N_Z))
        remote(own.at[0], there, os.at[i], orr.at[i], other).wait_recv()
    for i, step in enumerate(J_STEPS):
        copy = remote(row_of(j), row_of(j), gs.at[i], gr.at[i], (z * N_J + near(step), y))
        copy.start()
        sends.append(copy)
    def enter(b, _):
        table[b] = number_of(home_ref[b])
        return 0

    lax.fori_loop(0, NB, enter, 0, unroll=8)

    def numbers(lanes, row_at):
        chosen = jnp.where(iota((2 * TEAM * TILES_DEV * 4, lanes), 0) == row_at, 1.0, 0.0)
        logical = dot32(pairs_vec[...].astype(f32).astype(bf16), chosen.astype(bf16))
        home = jnp.broadcast_to(number_of(home_vec[...]), (8, NB)).astype(f32).astype(bf16)
        stored = []
        for k in range(2):
            match = jnp.where(iota((NB, lanes), 0).astype(f32) == logical[k : k + 1], 1.0, 0.0)
            stored.append(dot32(home, match.astype(bf16))[0:1])
        return stored

    r = iota((8 * N_J * N_Z, 1), 0)
    row_key = (((r // 8) * BLK_DEV + r % 4) * 2 + (r % 8) // 4).astype(f32)

    def one_hot(key):
        return jnp.where(row_key == key, 1.0, 0.0).astype(bf16)

    lanes = TEAM * TILES_DEV
    k = iota((1, lanes), 1)
    stored = numbers(lanes, ((k // 32) * N_J + j) * 32 + k % 32)
    for kc in range(4):
        pick[:, lanes * kc : lanes * (kc + 1)] = one_hot(stored[kc // 2] * 2.0 + kc % 2)
    late = TEAM * LATE
    k = iota((1, 4 * late), 1)
    m, t = (k % late) // LATE, EARLY + k % LATE
    stored = numbers(4 * late, ((m // N_Y) * N_J + j) * 32 + (m % N_Y) * TILES_DEV + t)
    key = jnp.where(k < 2 * late, stored[0], stored[1]) * 2.0 + ((k // late) % 2).astype(f32)
    final_pick[...] = one_hot(key)
    for m in range(TEAM):
        team[m, EARLY:] = jnp.zeros((LATE, 4, LANES), f32)
    for i, step in enumerate(J_STEPS):
        row = row_of(near(step, -1))
        remote(row, row, gs.at[i], gr.at[i], other).wait_recv()

    parts = ((0, 2), (2, 2), (4, TILES_DEV - 4))

    def block_of(tz, ty, t, k):
        row = (tz * N_J + j) * 32 + ty * TILES_DEV + t
        return table[pairs_ref[k, row]]

    def ask(i, g):
        at = pl.ds(*parts[g])
        return remote(pack.at[i, at], named.at[me, at], ts.at[g, i], tr.at[g, i], mate(i)[3])

    def asked(i, g):
        at = pl.ds(*parts[g])
        member = mate_from(i)[1]
        return remote(pack.at[i, at], named.at[member, at], ts.at[g, i], tr.at[g, i], other)

    for g, (t0, count) in enumerate(parts):

        def send(i, g=g, t0=t0, count=count):
            tz, ty, _, _ = mate(i)
            for t in range(t0, t0 + count):
                for k in range(2):
                    pack[i, t, 2 * k : 2 * k + 2, :] = grid[block_of(tz, ty, t, k)]
            ask(i, g).start()

        for i in MATES:
            send(i)
    for t in range(TILES_DEV):
        for k in range(2):
            named[me, t, 2 * k : 2 * k + 2, :] = grid[block_of(z, y, t, k)]

    lots = ((0, 4), (4, EARLY - 4), (EARLY, LATE))

    def give(i, g):
        at = pl.ds(*lots[g])
        _, _, member, to = mate(i)
        there = team.at[me, at] if g < 2 else final_team.at[me]
        return remote(part.at[member, at], there, ps.at[g, i], pr.at[g, i], to)

    def given(i, g):
        at = pl.ds(*lots[g])
        member = mate_from(i)[1]
        here = team.at[member, at] if g < 2 else final_team.at[member]
        return remote(part.at[0, at], here, ps.at[g, i], pr.at[g, i], other)

    def give_all(g):
        for dy in (2, 1, 3, 0):

            @pl.when(wrap(y + dy, N_Y) < 3)
            def _(dy=dy):
                for i in MATES:
                    if i % N_Y == dy:
                        give(i, g).start()

    def wait_asked(g):
        def wait(i, _):
            asked(i, g).wait_recv()
            return 0

        lax.fori_loop(1, TEAM, wait, 0)

    def two_tiles(pair, _):
        t = 2 * pair
        for g, (t0, _count) in enumerate(parts):
            pl.when(t == t0)(functools.partial(wait_asked, g))

        def rows(t, k):
            pieces = []
            for e in range(N_Z):
                pairs_of = [named[e * N_Y + q, t, 2 * k : 2 * k + 2, :] for q in range(N_Y)]
                pieces.append(jnp.concatenate(pairs_of, 0))
            return jnp.concatenate(pieces, 1)

        rates = [tile_rates(rows(t + u, 0), rows(t + u, 1), 128) for u in range(2)]
        for u in range(2):
            v1, s1, v2, s2 = rates[u]
            for k, v, st in ((0, v1, s1), (1, v2, s2)):
                full = jnp.concatenate([v, st], 0)
                for q in range(3):
                    for e in range(N_Z):
                        piece = full[2 * q : 2 * q + 2, LANES * e : LANES * (e + 1)]
                        part[e * N_Y + q, t + u, 2 * k : 2 * k + 2, :] = piece
        for g, (t0, count) in enumerate(lots):
            pl.when(t + 2 == t0 + count)(functools.partial(give_all, g))
        return 0

    lax.fori_loop(0, TILES_DEV // 2, two_tiles, 0)

    def by_block(chosen, terms):
        sums = dot32(chosen, jnp.concatenate(split3(terms), 1))
        return sums[:, 0:LANES] + (sums[:, LANES : 2 * LANES] + sums[:, 2 * LANES :])

    @pl.when(active)
    def _():
        team[me, 0:EARLY] = part[me, 0:EARLY]
        final_team[me] = part[me, EARLY:]

        def wait(g, i, _):
            given(i, g).wait_recv()
            return 0

        lax.fori_loop(1, TEAM, functools.partial(wait, 0), 0)
        lax.fori_loop(1, TEAM, functools.partial(wait, 1), 0)
        lanes = TEAM * TILES_DEV
        terms = jnp.concatenate([team[:, :, kc, :].reshape(lanes, LANES) for kc in range(4)], 0)
        sums = by_block(pick[...], terms)
        lax.fori_loop(1, TEAM, functools.partial(wait, 2), 0)
        terms = [final_team[:, :, kc, :].reshape(TEAM * LATE, LANES) for kc in range(4)]
        terms = jnp.concatenate(terms, 0)
        sums = sums + by_block(final_pick[...], terms)
        dense[...] = sums.reshape(N_J, N_Z, 8, LANES)
        for i, step in enumerate(J_STEPS):
            tj = near(step)
            remote(dense.at[tj], jin.at[i], js.at[i], jr.at[i], (z * N_J + tj, y)).start()
        for i in range(7):
            remote(dense.at[0], jin.at[i], js.at[i], jr.at[i], other).wait_recv()
        total = dense[j]
        for i in range(7):
            total = total + jin[i]
        dense[j] = total
        fin[me] = dense[j, z]

        for i in MATES:
            tz, _, _, to = mate(i)
            remote(dense.at[j, tz], fin.at[me], fs.at[i], fr.at[i], to).start()

    def settle(i, _):
        for g in range(3):
            ask(i, g).wait_send()

        @pl.when(mate(i)[1] < 3)
        def _():
            for g in range(3):
                give(i, g).wait_send()

        return 0

    lax.fori_loop(1, TEAM, settle, 0)
    for copy in sends:
        copy.wait_send()

    @pl.when(active)
    def _():
        for i, step in enumerate(J_STEPS):
            remote(dense.at[near(step)], jin.at[i], js.at[i], jr.at[i], other).wait_send()

    def last(i, _):
        from_y, member = mate_from(i)

        @pl.when(from_y < 3)
        def _():
            remote(dense.at[0, 0], fin.at[member], fs.at[i], fr.at[i], other).wait_recv()

        @pl.when(active)
        def _():
            tz, _, _, to = mate(i)
            remote(dense.at[j, tz], fin.at[me], fs.at[i], fr.at[i], to).wait_send()

        return 0

    lax.fori_loop(1, TEAM, last, 0)
    outs = [(vel_out, 0), (vel_out, 1), (vel_out, 2), (str_out, 0), (str_out, 1), (str_out, 2)]
    for q in range(3):
        for e in range(N_Z):
            full = fin[e * N_Y + q]
            for c in range(2):
                ref, row = outs[2 * q + c]
                for b in range(BLK_DEV):
                    at = slice(b * BS + e * LANES, b * BS + (e + 1) * LANES)
                    ref[row : row + 1, at] = full[c * 4 + b : c * 4 + b + 1]


def run(pairs, home, positions, strengths, radii):
    vmem, smem = pl.BlockSpec(memory_space=pltpu.VMEM), pl.BlockSpec(memory_space=pltpu.SMEM)
    dma = pltpu.SemaphoreType.DMA
    out = jax.ShapeDtypeStruct((3, BLK_DEV * BS), f32)
    n = BLK_DEV * BS
    words = [(2, 2 * TEAM * TILES_DEV * 4), (1, NB)]
    buffers = [
        (3, n),
        (3, n),
        (1, n),
        (N_Y, 2, BLK_DEV * BS),
        (N_Z, BLK_DEV, 2, LANES),
        (NB, 2, LANES),
        (TEAM, TILES_DEV, 4, LANES),
        (TEAM, TILES_DEV, 4, LANES),
        (TEAM, TILES_DEV, 4, LANES),
        (TEAM, TILES_DEV, 4, LANES),
        (TEAM, LATE, 4, LANES),
        (N_J, N_Z, 8, LANES),
        (7, N_Z, 8, LANES),
        (TEAM, 8, LANES),
    ]
    chosen = [(8 * N_J * N_Z, 4 * TEAM * TILES_DEV), (8 * N_J * N_Z, 4 * TEAM * LATE)]
    counts = [(7,), (7,), (3, TEAM), (3, TEAM), (7,), (TEAM,)]
    return pl.pallas_call(
        kernel,
        out_shape=(out, out),
        in_specs=[smem, smem] + [pl.BlockSpec(memory_space=pl.ANY)] * 5,
        out_specs=(vmem, vmem),
        scratch_shapes=[pltpu.SMEM((NB,), jnp.int32)]
        + [pltpu.VMEM(b, jnp.int32) for b in words]
        + [pltpu.VMEM(b, f32) for b in buffers]
        + [pltpu.VMEM(b, bf16) for b in chosen]
        + [dma((5,))]
        + [dma(c) for c in counts for _ in range(2)],
        compiler_params=pltpu.CompilerParams(
            collective_id=0, has_side_effects=True, vmem_limit_bytes=63 * 2**20
        ),
    )(pairs, home, pairs, home[None, :], positions, strengths, radii)


def body(positions, strengths, core_radii, tile_pairs, block_home):
    return run(tile_pairs.T, block_home, positions, strengths, core_radii[None, :])


def solution(mesh):
    return jax.shard_map(
        body,
        mesh=mesh,
        in_specs=(P(None, "gx"), P(None, "gx"), P("gx"), P(), P()),
        out_specs=(P(None, "gx"), P(None, "gx")),
        check_vma=False,
    )
```

```python
import functools

import jax
import jax.numpy as jnp
from jax import lax
from jax.experimental import pallas as pl
from jax.experimental.pallas import tpu as pltpu
from jax.sharding import PartitionSpec as P

BS = 1024
TILES_DEV = 8
BLK_DEV = 4
N_Z, N_X, N_CORE, N_Y = 8, 4, 2, 4
N_J = N_X * N_CORE
TEAM = N_Z * N_Y
SLOTS = 2 * TILES_DEV
NB = 256
ROW = BLK_DEV * N_Z
EARLY = TILES_DEV - 2
LATE = TILES_DEV - EARLY
LANES = 128
MESH = pl.DeviceIdType.MESH

inv_four_pi = 0.07957747154594767
f32, bf16 = jnp.float32, jnp.bfloat16
NT = (((1,), (1,)), ((), ()))
NN = (((1,), (0,)), ((), ()))


def split3(a):
    hi = a.astype(bf16)
    rest = a - hi.astype(f32)
    mid = rest.astype(bf16)
    lo = (rest - mid.astype(f32)).astype(bf16)
    return hi, mid, lo


def split2(v):
    hi = v.astype(bf16)
    return hi, (v - hi.astype(f32)).astype(bf16)


def cross_rows(a, b):
    a0, a1, a2 = (a[k : k + 1] for k in range(3))
    b0, b1, b2 = (b[k : k + 1] for k in range(3))
    return jnp.concatenate([a1 * b2 - a2 * b1, a2 * b0 - a0 * b2, a0 * b1 - a1 * b0], 0)


def moments(x, w):
    base = jnp.concatenate([w, cross_rows(x, w), jnp.zeros((2, w.shape[1]), f32)], 0)
    parts = [base] + [x[k : k + 1] * base for k in range(3)]
    full = split3(jnp.concatenate(parts, 0))
    return jnp.concatenate([s[:8] for s in full], 0), jnp.concatenate(full, 0)


def gains(x, w, a, s):
    a = a[0:8] + (a[8:16] + a[16:24])
    s = s[0:32] + (s[32:64] + s[64:96])
    along = x[0:1] * w[0:1] + x[1:2] * w[1:2] + x[2:3] * w[2:3]
    t = along * s[0:8] - (w[0:1] * s[8:16] + w[1:2] * s[16:24] + w[2:3] * s[24:32])
    vel = (cross_rows(x, a[0:3]) - a[3:6]) * -inv_four_pi
    turn = cross_rows(x, t[0:3]) - t[3:6]
    stretch = (3.0 * inv_four_pi) * turn - inv_four_pi * cross_rows(w, a[0:3])
    return vel, stretch


def tile_rates(first, second, piece):
    n = first.shape[1]
    total = jnp.sum(first[0:3], axis=1, keepdims=True) + jnp.sum(second[0:3], axis=1, keepdims=True)
    centre = total * (0.5 / n)
    xp, xq = first[0:3] - centre, second[0:3] - centre
    wp, wq = first[3:6], second[3:6]
    sp, sq = 0.5 * first[6:7] * first[6:7], 0.5 * second[6:7] * second[6:7]
    bp, mp = moments(xp, wp)
    bq, mq = moments(xq, wq)
    cols = jnp.transpose(jnp.concatenate([first[0:3], sp, first[4:8]], 0))
    aq = jnp.zeros((24, n), f32)
    hq = jnp.zeros((96, n), f32)
    ap, hp = [], []
    dot = functools.partial(lax.dot_general, preferred_element_type=f32)
    for s in range(0, n, piece):
        cs = cols[s : s + piece]
        r = [cs[:, k : k + 1] - second[k : k + 1] for k in range(3)]
        g = r[0] * r[0] + r[1] * r[1] + r[2] * r[2] + (cs[:, 3:4] + sq)
        q = lax.rsqrt(g)
        q2 = q * q
        f = q2 * q
        h = f * q2
        fh, fl = split2(f)
        hh, hl = split2(h)
        f2, h2 = jnp.concatenate([fh, fl], 0), jnp.concatenate([hh, hl], 0)
        both = dot(f2, bq, NT)
        ap.append(both[:piece] + both[piece:])
        both = dot(h2, mq, NT)
        hp.append(both[:piece] + both[piece:])
        bps, mps = bp[:, s : s + piece], mp[:, s : s + piece]
        aq = aq + dot(jnp.concatenate([bps, bps], 1), f2, NN)
        hq = hq + dot(jnp.concatenate([mps, mps], 1), h2, NN)
    ap, hp = jnp.transpose(jnp.concatenate(ap, 0)), jnp.transpose(jnp.concatenate(hp, 0))
    return gains(xp, wp, ap, hp) + gains(xq, wq, aq, hq)


def place():
    gx, y = lax.axis_index("gx"), lax.axis_index("gy")
    return gx // N_J, lax.rem(gx, N_J), y


def wrap(v, n):
    return lax.rem(v + n, n)


J_STEPS = [(2, 0), (2, 1), (1, 0), (3, 0), (1, 1), (3, 1), (0, 1)]
Z_STEPS = [4, 3, 5, 2, 6, 1, 7]
MATES = [dz * N_Y + dy for dz in Z_STEPS + [0] for dy in (2, 1, 3, 0) if dz or dy]


def remote(src, dst, send, recv, device):
    return pltpu.make_async_remote_copy(
        src_ref=src, dst_ref=dst, send_sem=send, recv_sem=recv, device_id=device, device_id_type=MESH
    )


def number_of(storage):
    z, j = lax.shift_right_logical(storage, 5), lax.shift_right_logical(storage, 2) & (N_J - 1)
    return j * ROW + z * BLK_DEV + (storage & (BLK_DEV - 1))


def iota(shape, axis):
    return lax.broadcasted_iota(jnp.int32, shape, axis)


def dot32(a, b):
    return lax.dot_general(a, b, NN, preferred_element_type=f32)


def kernel(
    pairs_ref, home_ref, pairs_hbm, home_hbm, pos_hbm, str_hbm, rad_hbm, vel_out, str_out,
    table, pairs_vec, home_vec, pos_ref, str_ref, rad_ref, mix, own, grid, pack, named, part, team, final_team, dense, jin, fin, pick, final_pick,
    loads, os, orr, gs, gr, ts, tr, ps, pr, js, jr, fs, fr,
):
    z, j, y = place()
    x, core = j // 2, lax.rem(j, 2)
    gx = z * N_J + j
    me = z * N_Y + y
    other = (gx, wrap(y + 1, N_Y))
    active = y < 3

    def mate(i):
        tz, ty = wrap(z + i // N_Y, N_Z), wrap(y + i % N_Y, N_Y)
        return tz, ty, tz * N_Y + ty, (tz * N_J + j, ty)

    def mate_from(i):
        tz, ty = wrap(z - i // N_Y, N_Z), wrap(y - i % N_Y, N_Y)
        return ty, tz * N_Y + ty

    def near(step, way=1):
        dx, dc = step
        return wrap(x + way * dx, N_X) * 2 + lax.rem(core + dc, 2)

    incoming = [(pos_hbm, pos_ref), (str_hbm, str_ref), (rad_hbm, rad_ref)]
    incoming += [(pairs_hbm, pairs_vec), (home_hbm, home_vec)]
    incoming = [pltpu.make_async_copy(a, b, loads.at[i]) for i, (a, b) in enumerate(incoming)]
    for copy in incoming:
        copy.start()
    barrier = pltpu.get_barrier_semaphore()
    greeted = [(wrap(z + dz, N_Z) * N_J + j, y) for dz in Z_STEPS]
    greeted += [(gx, wrap(y + dy, N_Y)) for dy in (2, 1, 3)]
    greeted += [(z * N_J + near(step), y) for step in J_STEPS]
    for to in greeted:
        pl.semaphore_signal(barrier, inc=1, device_id=to, device_id_type=MESH)


    for copy in incoming:
        copy.wait()
    rows_of = [(pos_ref, 0), (pos_ref, 1), (pos_ref, 2), (str_ref, 0), (str_ref, 1), (str_ref, 2)]
    for k, (ref, row) in enumerate(rows_of + [(rad_ref, 0)]):
        mix[k // 2, k % 2 : k % 2 + 1, :] = ref[row : row + 1, :]
    mix[3, 1:2, :] = jnp.zeros((1, BLK_DEV * BS), f32)
    for tz in range(N_Z):
        for b in range(BLK_DEV):
            own[tz, b] = mix[y, :, b * BS + tz * LANES : b * BS + (tz + 1) * LANES]

    pl.semaphore_wait(barrier, len(greeted))

    def home_of(tj, tz):
        return grid.at[pl.ds(tj * ROW + tz * BLK_DEV, BLK_DEV)]

    def row_of(tj):
        return grid.at[pl.ds(tj * ROW, ROW)]

    sends = []
    for i, dz in enumerate(Z_STEPS):
        tz = wrap(z + dz, N_Z)
        copy = remote(own.at[tz], home_of(j, z), os.at[i], orr.at[i], (tz * N_J + j, y))
        copy.start()
        sends.append(copy)
    for b in range(BLK_DEV):
        grid[j * ROW + z * BLK_DEV + b] = own[z, b]
    for i, dz in enumerate(Z_STEPS):
        there = home_of(j, wrap(z - dz, N_Z))
        remote(own.at[0], there, os.at[i], orr.at[i], other).wait_recv()
    for i, step in enumerate(J_STEPS):
        copy = remote(row_of(j), row_of(j), gs.at[i], gr.at[i], (z * N_J + near(step), y))
        copy.start()
        sends.append(copy)
    def enter(b, _):
        table[b] = number_of(home_ref[b])
        return 0

    lax.fori_loop(0, NB, enter, 0, unroll=8)

    def numbers(lanes, row_at):
        chosen = jnp.where(iota((2 * TEAM * TILES_DEV * 4, lanes), 0) == row_at, 1.0, 0.0)
        logical = dot32(pairs_vec[...].astype(f32).astype(bf16), chosen.astype(bf16))
        home = jnp.broadcast_to(number_of(home_vec[...]), (8, NB)).astype(f32).astype(bf16)
        stored = []
        for k in range(2):
            match = jnp.where(iota((NB, lanes), 0).astype(f32) == logical[k : k + 1], 1.0, 0.0)
            stored.append(dot32(home, match.astype(bf16))[0:1])
        return stored

    r = iota((8 * N_J * N_Z, 1), 0)
    row_key = (((r // 8) * BLK_DEV + r % 4) * 2 + (r % 8) // 4).astype(f32)

    def one_hot(key):
        return jnp.where(row_key == key, 1.0, 0.0).astype(bf16)

    lanes = TEAM * TILES_DEV
    k = iota((1, lanes), 1)
    stored = numbers(lanes, ((k // 32) * N_J + j) * 32 + k % 32)
    for kc in range(4):
        pick[:, lanes * kc : lanes * (kc + 1)] = one_hot(stored[kc // 2] * 2.0 + kc % 2)
    late = TEAM * LATE
    k = iota((1, 4 * late), 1)
    m, t = (k % late) // LATE, EARLY + k % LATE
    stored = numbers(4 * late, ((m // N_Y) * N_J + j) * 32 + (m % N_Y) * TILES_DEV + t)
    key = jnp.where(k < 2 * late, stored[0], stored[1]) * 2.0 + ((k // late) % 2).astype(f32)
    final_pick[...] = one_hot(key)
    for m in range(TEAM):
        team[m, EARLY:] = jnp.zeros((LATE, 4, LANES), f32)
    for i, step in enumerate(J_STEPS):
        row = row_of(near(step, -1))
        remote(row, row, gs.at[i], gr.at[i], other).wait_recv()

    parts = ((0, 2), (2, 2), (4, TILES_DEV - 4))

    def block_of(tz, ty, t, k):
        row = (tz * N_J + j) * 32 + ty * TILES_DEV + t
        return table[pairs_ref[k, row]]

    def ask(i, g):
        at = pl.ds(*parts[g])
        return remote(pack.at[i, at], named.at[me, at], ts.at[g, i], tr.at[g, i], mate(i)[3])

    def asked(i, g):
        at = pl.ds(*parts[g])
        member = mate_from(i)[1]
        return remote(pack.at[i, at], named.at[member, at], ts.at[g, i], tr.at[g, i], other)

    for g, (t0, count) in enumerate(parts):

        def fill(i, t0=t0, count=count):
            tz, ty, _, _ = mate(i)
            for t in range(t0, t0 + count):
                for k in range(2):
                    pack[i, t, 2 * k : 2 * k + 2, :] = grid[block_of(tz, ty, t, k)]

        for first in range(0, len(MATES), 8):
            for i in MATES[first : first + 8]:
                fill(i)
            for i in MATES[first : first + 8]:
                ask(i, g).start()
    for t in range(TILES_DEV):
        for k in range(2):
            named[me, t, 2 * k : 2 * k + 2, :] = grid[block_of(z, y, t, k)]

    lots = ((0, 4), (4, EARLY - 4), (EARLY, LATE))

    def give(i, g):
        at = pl.ds(*lots[g])
        _, _, member, to = mate(i)
        there = team.at[me, at] if g < 2 else final_team.at[me]
        return remote(part.at[member, at], there, ps.at[g, i], pr.at[g, i], to)

    def given(i, g):
        at = pl.ds(*lots[g])
        member = mate_from(i)[1]
        here = team.at[member, at] if g < 2 else final_team.at[member]
        return remote(part.at[0, at], here, ps.at[g, i], pr.at[g, i], other)

    def give_all(g):
        for dy in (2, 1, 3, 0):

            @pl.when(wrap(y + dy, N_Y) < 3)
            def _(dy=dy):
                for i in MATES:
                    if i % N_Y == dy:
                        give(i, g).start()

    def wait_asked(g):
        def wait(i, _):
            asked(i, g).wait_recv()
            return 0

        lax.fori_loop(1, TEAM, wait, 0)

    def two_tiles(pair, _):
        t = 2 * pair
        for g, (t0, _count) in enumerate(parts):
            pl.when(t == t0)(functools.partial(wait_asked, g))

        def rows(t, k):
            pieces = []
            for e in range(N_Z):
                pairs_of = [named[e * N_Y + q, t, 2 * k : 2 * k + 2, :] for q in range(N_Y)]
                pieces.append(jnp.concatenate(pairs_of, 0))
            return jnp.concatenate(pieces, 1)

        rates = [tile_rates(rows(t + u, 0), rows(t + u, 1), 128) for u in range(2)]
        for u in range(2):
            v1, s1, v2, s2 = rates[u]
            for k, v, st in ((0, v1, s1), (1, v2, s2)):
                full = jnp.concatenate([v, st], 0)
                for q in range(3):
                    for e in range(N_Z):
                        piece = full[2 * q : 2 * q + 2, LANES * e : LANES * (e + 1)]
                        part[e * N_Y + q, t + u, 2 * k : 2 * k + 2, :] = piece
        for g, (t0, count) in enumerate(lots):
            pl.when(t + 2 == t0 + count)(functools.partial(give_all, g))
        return 0

    lax.fori_loop(0, TILES_DEV // 2, two_tiles, 0)

    def by_block(chosen, terms):
        sums = dot32(chosen, jnp.concatenate(split3(terms), 1))
        return sums[:, 0:LANES] + (sums[:, LANES : 2 * LANES] + sums[:, 2 * LANES :])

    @pl.when(active)
    def _():
        team[me, 0:EARLY] = part[me, 0:EARLY]
        final_team[me] = part[me, EARLY:]

        def wait(g, i, _):
            given(i, g).wait_recv()
            return 0

        lax.fori_loop(1, TEAM, functools.partial(wait, 0), 0)
        lax.fori_loop(1, TEAM, functools.partial(wait, 1), 0)
        lanes = TEAM * TILES_DEV
        terms = jnp.concatenate([team[:, :, kc, :].reshape(lanes, LANES) for kc in range(4)], 0)
        sums = by_block(pick[...], terms)
        lax.fori_loop(1, TEAM, functools.partial(wait, 2), 0)
        terms = [final_team[:, :, kc, :].reshape(TEAM * LATE, LANES) for kc in range(4)]
        terms = jnp.concatenate(terms, 0)
        sums = sums + by_block(final_pick[...], terms)
        dense[...] = sums.reshape(N_J, N_Z, 8, LANES)
        for i, step in enumerate(J_STEPS):
            tj = near(step)
            remote(dense.at[tj], jin.at[i], js.at[i], jr.at[i], (z * N_J + tj, y)).start()
        for i in range(7):
            remote(dense.at[0], jin.at[i], js.at[i], jr.at[i], other).wait_recv()
        total = dense[j]
        for i in range(7):
            total = total + jin[i]
        dense[j] = total
        fin[me] = dense[j, z]

        for i in MATES:
            tz, _, _, to = mate(i)
            remote(dense.at[j, tz], fin.at[me], fs.at[i], fr.at[i], to).start()

    def settle(i, _):
        for g in range(3):
            ask(i, g).wait_send()

        @pl.when(mate(i)[1] < 3)
        def _():
            for g in range(3):
                give(i, g).wait_send()

        return 0

    lax.fori_loop(1, TEAM, settle, 0)
    for copy in sends:
        copy.wait_send()

    @pl.when(active)
    def _():
        for i, step in enumerate(J_STEPS):
            remote(dense.at[near(step)], jin.at[i], js.at[i], jr.at[i], other).wait_send()

    def last(i, _):
        from_y, member = mate_from(i)

        @pl.when(from_y < 3)
        def _():
            remote(dense.at[0, 0], fin.at[member], fs.at[i], fr.at[i], other).wait_recv()

        @pl.when(active)
        def _():
            tz, _, _, to = mate(i)
            remote(dense.at[j, tz], fin.at[me], fs.at[i], fr.at[i], to).wait_send()

        return 0

    lax.fori_loop(1, TEAM, last, 0)
    outs = [(vel_out, 0), (vel_out, 1), (vel_out, 2), (str_out, 0), (str_out, 1), (str_out, 2)]
    for q in range(3):
        for e in range(N_Z):
            full = fin[e * N_Y + q]
            for c in range(2):
                ref, row = outs[2 * q + c]
                for b in range(BLK_DEV):
                    at = slice(b * BS + e * LANES, b * BS + (e + 1) * LANES)
                    ref[row : row + 1, at] = full[c * 4 + b : c * 4 + b + 1]


def run(pairs, home, positions, strengths, radii):
    vmem, smem = pl.BlockSpec(memory_space=pltpu.VMEM), pl.BlockSpec(memory_space=pltpu.SMEM)
    dma = pltpu.SemaphoreType.DMA
    out = jax.ShapeDtypeStruct((3, BLK_DEV * BS), f32)
    n = BLK_DEV * BS
    words = [(2, 2 * TEAM * TILES_DEV * 4), (1, NB)]
    buffers = [
        (3, n),
        (3, n),
        (1, n),
        (N_Y, 2, BLK_DEV * BS),
        (N_Z, BLK_DEV, 2, LANES),
        (NB, 2, LANES),
        (TEAM, TILES_DEV, 4, LANES),
        (TEAM, TILES_DEV, 4, LANES),
        (TEAM, TILES_DEV, 4, LANES),
        (TEAM, TILES_DEV, 4, LANES),
        (TEAM, LATE, 4, LANES),
        (N_J, N_Z, 8, LANES),
        (7, N_Z, 8, LANES),
        (TEAM, 8, LANES),
    ]
    chosen = [(8 * N_J * N_Z, 4 * TEAM * TILES_DEV), (8 * N_J * N_Z, 4 * TEAM * LATE)]
    counts = [(7,), (7,), (3, TEAM), (3, TEAM), (7,), (TEAM,)]
    return pl.pallas_call(
        kernel,
        out_shape=(out, out),
        in_specs=[smem, smem] + [pl.BlockSpec(memory_space=pl.ANY)] * 5,
        out_specs=(vmem, vmem),
        scratch_shapes=[pltpu.SMEM((NB,), jnp.int32)]
        + [pltpu.VMEM(b, jnp.int32) for b in words]
        + [pltpu.VMEM(b, f32) for b in buffers]
        + [pltpu.VMEM(b, bf16) for b in chosen]
        + [dma((5,))]
        + [dma(c) for c in counts for _ in range(2)],
        compiler_params=pltpu.CompilerParams(
            collective_id=0, has_side_effects=True, vmem_limit_bytes=63 * 2**20
        ),
    )(pairs, home, pairs, home[None, :], positions, strengths, radii)


def body(positions, strengths, core_radii, tile_pairs, block_home):
    return run(tile_pairs.T, block_home, positions, strengths, core_radii[None, :])


def solution(mesh):
    return jax.shard_map(
        body,
        mesh=mesh,
        in_specs=(P(None, "gx"), P(None, "gx"), P("gx"), P(), P()),
        out_specs=(P(None, "gx"), P(None, "gx")),
        check_vma=False,
    )
```
